32 devices in a mesh: row: 4 (over x, core), seq: 8 (over z, y).
Axes of the slice: x: 2, y: 2, z: 4, core: 2. Of those that a mesh axis runs over, the one named last changes fastest.
Arguments:
- hidden: bfloat16 [4, 8192, 768], P('row', 'seq'), may hold values from -6 to 6
- lengths: int32 [4, 4], P('row'), may hold values from 0 to 8192, as said below
- cotangent: bfloat16 [4, 8192, 768], P('row', 'seq'), may hold values from -6 to 6
- norm_gain: bfloat16 [768], P(('row', 'seq')), may hold values from 0.099609375 to 1.8984375
- in_proj: bfloat16 [768, 3352], P(('row', 'seq')), may hold values from -0.21875 to 0.21875
- conv_weight: bfloat16 [4, 1792], P(None, ('row', 'seq')), may hold values from -3 to 3
- conv_bias: bfloat16 [1792], P(('row', 'seq')), may hold values from -0.5 to 0.5
- a_log: float32 [24], replicated, may hold values from -7 to 1
- dt_bias: float32 [24], replicated, may hold values from -6 to -3
- skip_weight: float32 [24], replicated, may hold values from 0.5 to 1.5
- inner_gain: bfloat16 [1536], P(('row', 'seq')), may hold values from 0.099609375 to 1.8984375
- out_proj: bfloat16 [1536, 768], P(('row', 'seq')), may hold values from -0.15625 to 0.15625
Outputs:
- block_out: bfloat16 [4, 8192, 768], P('row', 'seq')
- hidden_grad: bfloat16 [4, 8192, 768], P('row', 'seq')
- norm_gain_grad: float32 [768], P(('row', 'seq'))
- in_proj_grad: float32 [768, 3352], P(('row', 'seq'))
- conv_weight_grad: float32 [4, 1792], P(None, ('row', 'seq'))
- conv_bias_grad: float32 [1792], P(('row', 'seq'))
- a_log_grad: float32 [24], replicated
- dt_bias_grad: float32 [24], replicated
- skip_d_grad: float32 [24], replicated
- inner_gain_grad: float32 [1536], P(('row', 'seq'))
- out_proj_grad: float32 [1536, 768], P(('row', 'seq'))
The draws below stay inside these ranges and needn't reach their ends.
Inputs may be any that keep to these rules, and one draw needn't show every extreme that they name: Each row lists its sequences' lengths in order, each 2048 or more, and zeros only after the last sequence; a row's lengths add up to between half of 8192 and 8192, the rest of the row being padding. In each aligned group of 4 rows, one row holds a single sequence of 8192 positions and one row exactly two sequences; every other row holds two to four sequences.
All inputs are finite; a program needn't handle non-finite values.
Results may differ from the reference program's by a relative error of at most 0.0059.
Values may be sent and summed in bfloat16 or wider, within the bound.
A program may use at most 320 MiB of HBM per device.

```python
import jax
import jax.numpy as jnp
from jax import lax

MODEL_WIDTH = 768
MIXER_WIDTH = 1536
HEAD_COUNT = 24
HEAD_SIZE = 64
STATE = 128
CONV = 4
BLOCK = 256
ROW_LENGTH = 8192
LEAST_LENGTH = 2048
PACKED_ROWS = 4
SLOTS = 4
CHANNELS = 1792
PROJ = 3352


def draw_lengths(key, part):
    key = jax.random.fold_in(key, 11)
    group_size = 4
    groups = PACKED_ROWS // group_size
    most_count = min(SLOTS, 4)
    chosen = jax.random.randint(jax.random.fold_in(key, 1), (groups,), 0, group_size)
    place = jnp.arange(PACKED_ROWS, dtype=jnp.int32) % group_size
    picked = jnp.repeat(chosen, group_size)
    spanning_rows = place == picked
    paired_rows = place == (picked + 1) % group_size
    count_draw = jax.random.randint(jax.random.fold_in(key, 2), (PACKED_ROWS,), 2, most_count + 1)
    seq_count = jnp.where(paired_rows, 2, count_draw).astype(jnp.int32)
    spare = ROW_LENGTH - seq_count * LEAST_LENGTH
    least_extra = jnp.maximum(ROW_LENGTH // 2 - seq_count * LEAST_LENGTH, 0)
    extra_raw = jax.random.randint(jax.random.fold_in(key, 3), (PACKED_ROWS,), 0, 1 << 20)
    extra_total = least_extra + extra_raw % (spare - least_extra + 1)
    left_over = extra_total
    columns = []
    for slot in range(SLOTS):
        raw = jax.random.randint(jax.random.fold_in(key, 100 + slot), (PACKED_ROWS,), 0, 1 << 20)
        in_use = slot < seq_count
        is_last = seq_count - 1 == slot
        extra_here = jnp.where(is_last, left_over, raw % (left_over + 1))
        extra_here = jnp.where(in_use, extra_here, 0)
        length_value = jnp.where(in_use, LEAST_LENGTH + extra_here, 0)
        left_over = left_over - extra_here
        if slot == 0:
            length_value = jnp.where(spanning_rows, ROW_LENGTH, length_value)
        else:
            length_value = jnp.where(spanning_rows, 0, length_value)
        columns.append(length_value.astype(jnp.int32))
    return jnp.stack(columns, axis=1).astype(jnp.int32)


def block_levels(own_key, extent, shards, low, largest):
    loudness = 1.0
    for axis_at, blocks in shards:
        steps = jax.random.uniform(jax.random.fold_in(jax.random.fold_in(own_key, 6), axis_at), (blocks,), jnp.float32, low / len(shards), largest / len(shards))
        loudness = loudness * jnp.repeat(jnp.exp(steps), extent[axis_at] // blocks).reshape((-1,) + (1,) * (len(extent) - 1 - axis_at))
    return loudness


def centred(key, shape, deviation, most, pieces=(), kind=jnp.bfloat16):
    factor_of = block_levels(key, shape, pieces, -0.22, 0.18) if pieces else 1.0
    values = jax.random.normal(key, shape, jnp.float32) * deviation * factor_of
    return jnp.minimum(jnp.maximum(values, -most), most).astype(kind)


def setup_inputs(seed: int = 0) -> dict:
    key_list = jax.random.split(jax.random.key(seed), 13)
    return {
        "hidden": centred(key_list[0], (PACKED_ROWS, ROW_LENGTH, MODEL_WIDTH), 1.0, 6.0, ((0, 4), (1, 8))),
        "lengths": draw_lengths(jax.random.fold_in(key_list[12], 71), 0),
        "cotangent": centred(key_list[2], (PACKED_ROWS, ROW_LENGTH, MODEL_WIDTH), 1.0, 6.0, ((0, 4), (1, 8))),
        "norm_gain": jnp.clip(1.0 + 0.18 * jax.random.normal(key_list[3], (MODEL_WIDTH,), jnp.float32), 0.099609375, 1.8984375).astype(jnp.bfloat16),
        "in_proj": centred(key_list[4], (MODEL_WIDTH, PROJ), MODEL_WIDTH ** -0.5, 0.21875, ((0, 32),)),
        "conv_weight": centred(key_list[5], (CONV, CHANNELS), CONV ** -0.5, 3.0, ((1, 32),)),
        "conv_bias": jnp.clip(jax.random.uniform(key_list[6], (CHANNELS,), jnp.float32, -0.5, 0.5) * block_levels(key_list[6], (CHANNELS,), ((0, 32),), -0.4, 0.0), -0.5, 0.5).astype(jnp.bfloat16),
        "a_log": jnp.clip(jax.random.uniform(key_list[7], (HEAD_COUNT,), jnp.float32, -7.0, 1.0), -7.0, 1.0),
        "dt_bias": jnp.clip(jax.random.uniform(key_list[8], (HEAD_COUNT,), jnp.float32, -6.0, -3.0), -6.0, -3.0),
        "skip_weight": jnp.clip(jax.random.uniform(key_list[9], (HEAD_COUNT,), jnp.float32, 0.5, 1.5), 0.5, 1.5),
        "inner_gain": jnp.clip(1.0 + 0.18 * jax.random.normal(key_list[10], (MIXER_WIDTH,), jnp.float32), 0.099609375, 1.8984375).astype(jnp.bfloat16),
        "out_proj": centred(key_list[11], (MIXER_WIDTH, MODEL_WIDTH), MIXER_WIDTH ** -0.5, 0.15625, ((0, 32),)),
    }


EPS = 1e-05
HIGHEST = lax.Precision.HIGHEST

@jax.custom_vjp
def low(v):
    return lax.optimization_barrier(v.astype(jnp.bfloat16)).astype(jnp.float32)

@jax.custom_vjp
def low_back(v):
    return v

def low_keep(v):
    return (low(v), None)

def low_pass(kept, grad):
    return (grad,)

def back_keep(v):
    return (v, None)

def back_low(kept, grad):
    return (low(grad),)
low.defvjp(low_keep, low_pass)
low_back.defvjp(back_keep, back_low)

def segment_ids(lengths, position_index):
    ends = jnp.cumsum(lengths, axis=1).astype(jnp.int32)
    segment = lax.optimization_barrier(jnp.sum((ends[:, None, :] <= position_index[None, :, None]).astype(jnp.int32), axis=2)).astype(jnp.int32)
    valid = position_index[None, :] < ends[:, -1:]
    return (segment, valid)

def rms_scale(value_rows, gain):
    return value_rows * lax.rsqrt(lax.optimization_barrier(jnp.mean(value_rows * value_rows, axis=-1, keepdims=True)) + EPS) * gain

def gated_norm(mixer_layer, gate, gain):
    return rms_scale(mixer_layer * jax.nn.silu(gate), gain)

def causal_conv(padded, kernel, offset, segment):
    width = kernel.shape[0]
    length_value = padded.shape[1] - width + 1
    own = segment[:, width - 1:]
    total = offset
    for index in range(width):
        same = (segment[:, index:index + length_value] == own)[..., None]
        total = total + jnp.where(same, padded[:, index:index + length_value], 0.0) * kernel[index]
    return jax.nn.silu(total)

def rates(step_raw, dt_bias, a_log):
    step = jax.nn.softplus(step_raw + dt_bias)
    return (step, -step * jnp.exp(a_log))

def block_parts(value_rows, in_map, out_map, step, log_decay, segment, segment_prev):
    batch, length_value, heads, head_dim = value_rows.shape
    count = length_value // BLOCK
    blocked = value_rows.reshape(batch, count, BLOCK, heads, head_dim)
    inputs = in_map.reshape(batch, count, BLOCK, -1)
    readout = out_map.reshape(batch, count, BLOCK, -1)
    steps = step.reshape(batch, count, BLOCK, heads)
    running = jnp.cumsum(log_decay.reshape(batch, count, BLOCK, heads), axis=2)
    labels = segment.reshape(batch, count, BLOCK)
    before = jnp.concatenate([segment_prev[:, None], labels[:, :-1, -1]], axis=1)
    order = jnp.arange(BLOCK)
    inside = ((labels[:, :, :, None] == labels[:, :, None, :]) & (order[:, None] >= order[None, :]))[:, :, None]
    turned = jnp.moveaxis(running, 3, 2)
    spread = turned[..., :, None] - turned[..., None, :]
    decay = jnp.where(inside, jnp.exp(jnp.where(inside, spread, 0.0)), 0.0)
    scores = jnp.einsum('rkqn,rksn->rkqs', readout, inputs, precision=HIGHEST)
    mixing = decay * scores[:, :, None] * jnp.moveaxis(steps, 3, 2)[:, :, :, None, :]
    inner = jnp.einsum('rkhqs,rkshp->rkqhp', mixing, blocked, precision=HIGHEST)
    last = labels[:, :, -1]
    keep = (labels == last[:, :, None])[..., None]
    tail = jnp.where(keep, jnp.exp(jnp.where(keep, running[:, :, -1:, :] - running, 0.0)), 0.0) * steps
    local_state = jnp.einsum('rkshp,rksn->rkhpn', blocked * tail[..., None], inputs, precision=HIGHEST)
    carry = jnp.where((last == before)[..., None], jnp.exp(running[:, :, -1, :]), 0.0)
    entry = jnp.where((labels == before[:, :, None])[..., None], jnp.exp(running), 0.0)
    return (inner, local_state, carry, entry, readout)

def block_chain(local_state, carry, state_in):

    def advance(state, item):
        factor, fresh = item
        return (factor[:, :, None, None] * state + fresh, state)
    final, entering = lax.scan(advance, state_in, (jnp.moveaxis(carry, 1, 0), jnp.moveaxis(local_state, 1, 0)))
    return (final, jnp.moveaxis(entering, 0, 1))

def block_output(inner, entry, readout, entering):
    carried = entry[..., None] * jnp.einsum('rkqn,rkhpn->rkqhp', readout, entering, precision=HIGHEST)
    batch, count, width, heads, head_dim = inner.shape
    return (inner + carried).reshape(batch, count * width, heads, head_dim)

def ssm_output(value_rows, in_map, out_map, step_raw, dt_bias, a_log, segment, segment_prev, state_in):
    step, log_decay = rates(step_raw, dt_bias, a_log)
    inner, local_state, carry, entry, readout = block_parts(value_rows, in_map, out_map, step, log_decay, segment, segment_prev)
    final, entering = block_chain(local_state, carry, state_in)
    return block_output(inner, entry, readout, entering)

def row_forward(weights, hidden_row, length_row):
    norm_gain, in_proj, conv_weight, conv_bias, a_log, dt_bias, skip_weight, inner_gain, out_proj = weights
    channels = MIXER_WIDTH + 2 * STATE
    position_index = jnp.arange(ROW_LENGTH, dtype=jnp.int32)
    segment, valid = segment_ids(length_row[None], position_index)
    residual = hidden_row[None]
    normed = low(rms_scale(residual, norm_gain))
    projected = low_back(jnp.einsum('rtd,de->rte', normed, in_proj, precision=HIGHEST))
    gate = projected[..., :MIXER_WIDTH]
    mixed_in = projected[..., MIXER_WIDTH:MIXER_WIDTH + channels]
    step_raw = projected[..., MIXER_WIDTH + channels:]
    padded = jnp.concatenate([jnp.zeros((1, CONV - 1, channels), jnp.float32), mixed_in], axis=1)
    labels = jnp.concatenate([jnp.full((1, CONV - 1), -1, jnp.int32), segment], axis=1)
    active_flag = causal_conv(padded, conv_weight, conv_bias, labels)
    value_rows = active_flag[..., :MIXER_WIDTH].reshape(1, ROW_LENGTH, HEAD_COUNT, HEAD_SIZE)
    in_map = active_flag[..., MIXER_WIDTH:MIXER_WIDTH + STATE]
    out_map = active_flag[..., MIXER_WIDTH + STATE:]
    scanned_state = ssm_output(value_rows, in_map, out_map, step_raw, dt_bias, a_log, segment, jnp.full((1,), -1, jnp.int32), jnp.zeros((1, HEAD_COUNT, HEAD_SIZE, STATE), jnp.float32))
    mixer_layer = (scanned_state + skip_weight[:, None] * value_rows).reshape(1, ROW_LENGTH, MIXER_WIDTH)
    gated = low(gated_norm(mixer_layer, gate, inner_gain))
    branch = jnp.einsum('rti,id->rtd', gated, out_proj, precision=HIGHEST)
    return jnp.where(valid[..., None], residual + branch, 0.0)[0]

def reference(hidden, lengths, cotangent, norm_gain, in_proj, conv_weight, conv_bias, a_log, dt_bias, skip_weight, inner_gain, out_proj):
    weights = (norm_gain.astype(jnp.float32), in_proj.astype(jnp.float32), conv_weight.astype(jnp.float32), conv_bias.astype(jnp.float32), a_log.astype(jnp.float32), dt_bias.astype(jnp.float32), skip_weight.astype(jnp.float32), inner_gain.astype(jnp.float32), out_proj.astype(jnp.float32))

    def forward(weights_arg, hidden_arg):

        def one_row(item):
            return row_forward(weights_arg, item[0], item[1])
        return lax.map(jax.checkpoint(one_row), (hidden_arg, lengths))
    block_out, pull = jax.vjp(forward, weights, hidden.astype(jnp.float32))
    weight_grads, hidden_grad = pull(cotangent.astype(jnp.float32))
    return (block_out.astype(jnp.bfloat16), hidden_grad.astype(jnp.bfloat16), weight_grads[0], weight_grads[1], weight_grads[2], weight_grads[3], weight_grads[4], weight_grads[5], weight_grads[6], weight_grads[7], weight_grads[8])
```

```python
import functools

import jax
import jax.numpy as jnp
from jax import lax
from jax.experimental import pallas as pl
from jax.experimental.pallas import tpu as pltpu
from jax.sharding import PartitionSpec as P

BLOCK = 256
EPS = 1e-05
LOG2E = 1.4426950408889634
HIGHEST = lax.Precision.HIGHEST
F32 = jnp.float32
LOW = jnp.bfloat16
EDGE = 8
HALO = 16
AXES = ("row", "seq")
MESH = pl.DeviceIdType.MESH
CORES = 2
DEPTH = 4
VMEM_BYTES = 63 * 1024 * 1024


def nn(a, b, precision=None):
    return lax.dot_general(
        a, b, (((1,), (0,)), ((), ())), precision=precision, preferred_element_type=F32
    )


def nt(a, b):
    return lax.dot_general(a, b, (((1,), (1,)), ((), ())), preferred_element_type=F32)


def tn(a, b, precision=None):
    return lax.dot_general(
        a, b, (((0,), (0,)), ((), ())), precision=precision, preferred_element_type=F32
    )


def halves(v):
    high = v.astype(LOW)
    return high, (v - high.astype(F32)).astype(LOW)


def head_groups(heads, width):
    column = lax.broadcasted_iota(jnp.int32, (heads, width), 1)
    first = lax.broadcasted_iota(jnp.int32, (heads, width), 0) * (width // heads)
    return ((column >= first) & (column < first + width // heads)).astype(F32).astype(LOW)


def spread(v, groups):
    high, rest = halves(v)
    return nn(high, groups) + nn(rest, groups)


def head_sums(v, groups):
    high, rest = halves(v)
    return nt(high, groups) + nt(rest, groups)


def triangle():
    return (
        lax.broadcasted_iota(jnp.int32, (BLOCK, BLOCK), 0) >= lax.broadcasted_iota(jnp.int32, (BLOCK, BLOCK), 1)
    ).astype(F32)


def sigmoid(v):
    return 0.5 + 0.5 * jnp.tanh(0.5 * v)


def log1p_of(v):
    series = v * (1.0 - v * (0.5 - v * (1.0 / 3.0 - 0.25 * v)))
    return jnp.where(v < 0.01, series, jnp.log(1.0 + v))


def rms_rate(v):
    return lax.rsqrt(jnp.mean(v * v, axis=-1, keepdims=True) + EPS)


class Labels:
    def __init__(self, info, block, rows=BLOCK):
        slots = info.shape[1] - 1
        self.ends, total = [], 0
        for i in range(slots):
            total = total + info[0, i]
            self.ends.append(total)
        self.base = info[0, slots] + block * BLOCK
        self.rows = rows

    def of(self, place):
        total = sum((place >= end).astype(jnp.int32) for end in self.ends)
        return jnp.where(place < 0, -1, total)

    def column(self):
        return self.of(self.base + lax.broadcasted_iota(jnp.int32, (self.rows, 1), 0))

    def row(self):
        return self.of(self.base + lax.broadcasted_iota(jnp.int32, (1, self.rows), 1))

    def before(self):
        return self.of(self.base - 1)

    def last(self):
        return self.of(self.base + BLOCK - 1)

    def entry(self):
        return (self.column() == self.before()).astype(F32)

    def keep(self):
        return (self.column() == self.last()).astype(F32)

    def flag(self):
        return (jnp.full((8, 128), self.before(), jnp.int32) == self.last()).astype(F32)

    def valid(self):
        place = self.base + lax.broadcasted_iota(jnp.int32, (self.rows, 1), 0)
        return (place < self.ends[-1]).astype(F32)

    def same(self):
        shape = (self.rows, 8)
        place = self.base + lax.broadcasted_iota(jnp.int32, shape, 0)
        own = self.of(place)
        return (self.of(place - lax.broadcasted_iota(jnp.int32, shape, 1)) == own).astype(F32)


class Place:
    def __init__(self):
        rows, self.seqs = lax.axis_size("row"), lax.axis_size("seq")
        self.sx, self.sz = rows // CORES, DEPTH
        self.sy = self.seqs // DEPTH
        row, seq = lax.axis_index("row"), lax.axis_index("seq")
        self.x, self.core = lax.div(row, CORES), lax.rem(row, CORES)
        self.z, self.y = lax.div(seq, self.sy), lax.rem(seq, self.sy)
        self.row, self.seq = row, seq
        self.count = rows * self.seqs
        self.twin = self.device(core=1 - self.core)

    def device(self, x=None, core=None, z=None, y=None):
        x = self.x if x is None else x
        core = self.core if core is None else core
        z = self.z if z is None else z
        y = self.y if y is None else y
        return {"row": x * CORES + core, "seq": z * self.sy + y}

    def slot(self, x=None, core=None, z=None, y=None):
        at = self.device(x, core, z, y)
        return at["row"] * self.seqs + at["seq"]

    def peers(self, axis):
        size, mine = {"x": (self.sx, self.x), "y": (self.sy, self.y), "z": (self.sz, self.z)}[axis]
        return [(k, lax.rem(mine + k, size)) for k in range(1, size)]

    def around(self):
        return (
            [self.device(x=p) for _, p in self.peers("x")]
            + [self.device(y=p) for _, p in self.peers("y")]
            + [self.device(z=p) for _, p in self.peers("z")]
            + [self.twin]
        )

    def along(self, by):
        return {"seq": lax.rem(self.seq + by + self.seqs, self.seqs)}


def greet(devices):
    barrier = pltpu.get_barrier_semaphore()
    for device in devices:
        pl.semaphore_signal(barrier, inc=1, device_id=device, device_id_type=MESH)
    pl.semaphore_wait(barrier, len(devices))


def remote(source, target, send_sem, recv_sem, device):
    return pltpu.make_async_remote_copy(
        src_ref=source, dst_ref=target, send_sem=send_sem, recv_sem=recv_sem, device_id=device, device_id_type=MESH
    )


class Gather:
    def __init__(self, me, ins, outs, local_sem, send_sem, recv_sem):
        self.me, self.ins, self.outs = me, ins, outs
        self.local_sem, self.send_sem, self.recv_sem = local_sem, send_sem, recv_sem
        self.steps = [[self.plan(a, stage) for stage in range(4)] for a in range(len(ins))]

    def plan(self, a, stage):
        me = self.me
        xs = [p for _, p in me.peers("x")]
        ys = [p for _, p in me.peers("y")]
        zs = [p for _, p in me.peers("z")]
        around = [(me.device(y=p), None) for p in ys] + [(me.device(x=p), None) for p in xs] + [(me.twin, None)]
        if stage == 0:
            return [(None, [(me.device(z=p), None) for p in zs] + around)]
        if stage == 1:
            return [(me.slot(z=z), around) for z in zs]
        turns = [lax.rem(me.z + k, me.sz) for k in range(me.sz)]
        found = []
        for z in turns:
            even = lax.rem(z, 2) == 0
            if stage == 2:
                for y in ys:
                    found.append((me.slot(z=z, y=y), [(me.device(x=p), even) for p in xs] + [(me.twin, None)]))
                for x in xs:
                    found.append(
                        (me.slot(z=z, x=x), [(me.device(y=p), jnp.logical_not(even)) for p in ys] + [(me.twin, None)])
                    )
            else:
                for y in ys:
                    for x in xs:
                        found.append((me.slot(z=z, x=x, y=y), [(me.twin, None)]))
        return found

    def copies(self, a, stage):
        index = sum(len(to) for earlier in self.steps[a][:stage] for _, to in earlier)
        found = []
        for slot, to in self.steps[a][stage]:
            at = self.me.slot() if slot is None else slot
            source = self.ins[a] if slot is None else self.outs[a].at[at]
            group = []
            for device, when in to:
                group.append(
                    (remote(source, self.outs[a].at[at], self.send_sem.at[a, index], self.recv_sem.at[a, at], device), when)
                )
                index += 1
            found.append((slot, group))
        return found

    def arrived(self, a, slot):
        block = self.outs[a].at[slot]
        remote(block, block, self.send_sem.at[a, 0], self.recv_sem.at[a, slot], self.me.twin).wait_recv()

    def own(self, a):
        return pltpu.make_async_copy(self.ins[a], self.outs[a].at[self.me.slot()], self.local_sem.at[a])

    def run(self, stage):
        for a in range(len(self.ins)):
            if stage == 0:
                self.own(a).start()
            for slot, group in self.copies(a, stage):
                if slot is not None:
                    self.arrived(a, slot)
                for copy, when in group:
                    if when is None:
                        copy.start()
                    else:
                        pl.when(when)(copy.start)

    def finish(self):
        me = self.me
        for a in range(len(self.ins)):
            for x in range(me.sx):
                for seq in range(me.seqs):
                    self.arrived(a, (x * CORES + 1 - me.core) * me.seqs + seq)
            self.own(a).wait()
            for stage in range(4):
                for _, group in self.copies(a, stage):
                    for copy, when in group:
                        if when is None:
                            copy.wait_send()
                        else:
                            pl.when(when)(copy.wait_send)


def gather_semaphores(arrays):
    devices = lax.axis_size(AXES)
    return [
        pltpu.SemaphoreType.DMA((arrays,)),
        pltpu.SemaphoreType.DMA((arrays, 3 * devices)),
        pltpu.SemaphoreType.DMA((arrays, devices)),
    ]


class Exchange:
    def __init__(self, reverse, group, state, through, landed, out, parts, factors, ready, sems):
        self.reverse, self.group = reverse, group
        self.state, self.through, self.landed, self.out = state, through, landed, out
        self.parts, self.factors, self.ready, self.sems = parts, factors, ready, sems
        self.size, self.mine = lax.axis_size("seq"), lax.axis_index("seq")

    def copy(self, source, target, kind, index_out, index_in, peer):
        return remote(source, target, self.sems.at[kind, index_out], self.sems.at[kind + 1, index_in], {"seq": peer})

    def first(self):
        found = []
        for k in range(1, self.size):
            peer = lax.rem(self.mine + k, self.size)
            found.append(self.copy(self.through, self.factors.at[self.mine], 2, k, self.mine, peer))
            found.append(self.copy(self.state.at[peer], self.parts.at[self.mine], 0, k, self.mine, peer))
        return found

    def result(self, j):
        return self.copy(self.ready.at[j], self.out.at[self.mine], 4, j, self.mine, j)

    def start(self):
        greet([{"seq": lax.rem(self.mine + k, self.size)} for k in range(1, self.size)])
        for copy in self.first():
            copy.start()
        self.parts[self.mine] = self.state[self.mine]
        self.factors[self.mine] = self.through[...]

    def middle(self):
        group = self.group()
        heads = group.shape[0]
        total = jnp.zeros(self.state.shape[1:], F32)
        for k in range(self.size):
            j = self.size - 1 - k if self.reverse else k
            self.ready[j] = total.astype(LOW)

            @pl.when(self.mine != j)
            def _(j=j):
                self.result(j).start()
                self.copy(self.through, self.factors.at[j], 2, 0, j, j).wait_recv()
                self.copy(self.state.at[0], self.parts.at[j], 0, 0, j, j).wait_recv()

            factor = spread(self.factors[j][:, :heads], group)
            total = factor[0:1] * total + self.parts[j].astype(F32)
        self.out[self.mine] = self.ready[self.mine]

    def finish(self):
        for k in range(1, self.size):
            j = lax.rem(self.mine + k, self.size)
            self.copy(self.ready.at[j], self.out.at[j], 4, j, j, j).wait_recv()
        self.landed[...] = self.out[...]
        for copy in self.first():
            copy.wait_send()
        for j in range(self.size):
            pl.when(self.mine != j)(self.result(j).wait_send)


def exchange_scratch(pieces):
    size = pieces[0]
    return [
        pltpu.VMEM(pieces, LOW), pltpu.VMEM(pieces, LOW), pltpu.VMEM((size, 8, 128), F32), pltpu.VMEM(pieces, LOW),
        pltpu.SemaphoreType.DMA((6, size)),
    ]


def add_slots(target, first, source, pieces):
    def step(i, _):
        at = first + i
        target[at] = (target[at].astype(F32) + source[i].astype(F32)).astype(target.dtype)
        return 0

    lax.fori_loop(0, pieces, step, 0)


class Scatter:
    def __init__(self, me, sources, bufs, send_sem, recv_sem):
        self.me, self.sources, self.bufs = me, sources, bufs
        self.send_sem, self.recv_sem = send_sem, recv_sem
        self.order = [lax.rem(me.x + k, me.sx) for k in range(1, me.sx + 1)]
        self.even, self.odd = range(0, me.sz, 2), range(1, me.sz, 2)
        sx, sy, sz = me.sx, me.sy, me.sz
        self.base = [0, sx]
        for more in ((sx - 1) * sz, (sy - 1) * sx * sz, (sy - 1) * sz, (sx - 1) * sz):
            self.base.append(self.base[-1] + more)

    def plan(self, a, stage):
        me, base = self.me, self.base
        sx, sy, sz = me.sx, me.sy, me.sz
        twin_buf, total, from_x, from_y, from_y2, from_x2, from_z = self.bufs[a]
        xs, ys, zs = me.peers("x"), me.peers("y"), me.peers("z")
        found = []
        if stage == 0:
            for x in self.order:
                found.append((self.sources[a](x), twin_buf.at[x], x, me.twin))
        if stage == 1:
            for k, x in xs:
                for z in self.even:
                    found.append(
                        (
                            total.at[x, pl.ds(z * sy, sy)], from_x.at[k - 1, z], base[1] + (k - 1) * sz + z,
                            me.device(x=x),
                        )
                    )
            for k, y in ys:
                for z in self.odd:
                    for x in range(sx):
                        found.append(
                            (
                                total.at[x, z * sy + y], from_y.at[k - 1, x, z], base[2] + ((k - 1) * sx + x) * sz + z,
                                me.device(y=y),
                            )
                        )
        if stage == 2:
            for z in self.even:
                for k, y in ys:
                    found.append(
                        (total.at[me.x, z * sy + y], from_y2.at[k - 1, z], base[3] + (k - 1) * sz + z, me.device(y=y))
                    )
            for z in self.odd:
                for k, x in xs:
                    found.append(
                        (total.at[x, z * sy + me.y], from_x2.at[k - 1, z], base[4] + (k - 1) * sz + z, me.device(x=x))
                    )
        if stage == 3:
            for k, z in zs:
                found.append((total.at[me.x, z * sy + me.y], from_z.at[k - 1], base[5] + k - 1, me.device(z=z)))
        return found

    def copies(self, a, stage):
        me = self.me
        sx, sy = me.sx, me.sy
        ne, no = len(self.even), len(self.odd)
        counts = [sx, (sx - 1) * ne + (sy - 1) * no * sx, ne * (sy - 1) + no * (sx - 1)]
        index = sum(counts[:stage])
        return [
            remote(source, target, self.send_sem.at[a, index + i], self.recv_sem.at[a, arrival], device)
            for i, (source, target, arrival, device) in enumerate(self.plan(a, stage))
        ]

    def arrived(self, a, target, arrival):
        remote(target, target, self.send_sem.at[a, 0], self.recv_sem.at[a, arrival], self.me.twin).wait_recv()

    def send(self, a, stage):
        for copy in self.copies(a, stage):
            copy.start()

    def absorb(self, a, stage):
        me, base = self.me, self.base
        sx, sy, sz = me.sx, me.sy, me.sz
        twin_buf, total, from_x, from_y, from_y2, from_x2, from_z = self.bufs[a]
        if stage == 0:
            for x in self.order:
                self.arrived(a, twin_buf.at[x], x)
                add_slots(total.at[x], 0, twin_buf.at[x], me.seqs)
        if stage == 1:
            for k in range(1, sx):
                for z in self.even:
                    self.arrived(a, from_x.at[k - 1, z], base[1] + (k - 1) * sz + z)
                    add_slots(total.at[me.x], z * sy, from_x.at[k - 1, z], sy)
            for k in range(1, sy):
                for z in self.odd:
                    for x in range(sx):
                        self.arrived(a, from_y.at[k - 1, x, z], base[2] + ((k - 1) * sx + x) * sz + z)
                        add_slots(total.at[x], z * sy + me.y, from_y.at[k - 1, x, pl.ds(z, 1)], 1)
        if stage == 2:
            for z in range(sz):
                many, source, first = (sy, from_y2, base[3]) if z % 2 == 0 else (sx, from_x2, base[4])
                for k in range(1, many):
                    self.arrived(a, source.at[k - 1, z], first + (k - 1) * sz + z)
                    add_slots(total.at[me.x], z * sy + me.y, source.at[k - 1, pl.ds(z, 1)], 1)

    def result(self, a):
        me = self.me
        total, from_z = self.bufs[a][1], self.bufs[a][6]
        result = total[me.x, me.z * me.sy + me.y].astype(F32)
        for k in range(1, me.sz):
            self.arrived(a, from_z.at[k - 1], self.base[5] + k - 1)
            result = result + from_z[k - 1].astype(F32)
        return result

    def settle(self):
        for a in range(len(self.sources)):
            for stage in range(4):
                for copy in self.copies(a, stage):
                    copy.wait_send()


SCATTER_BUFFERS = 7


def scatter_scratch(ones, dtype=LOW):
    rows, seqs = lax.axis_size("row"), lax.axis_size("seq")
    sx, sz, sy = rows // CORES, DEPTH, seqs // DEPTH
    scratch = []
    for one in ones:
        for lead in ((sx, seqs), (sx, seqs), (sx - 1, sz, sy), (sy - 1, sx, sz), (sy - 1, sz), (sx - 1, sz), (sz - 1,)):
            scratch.append(pltpu.VMEM(lead + tuple(one), dtype))
    arrivals = sx + (sx - 1) * sz + (sy - 1) * sx * sz + (sy - 1) * sz + (sx - 1) * sz + sz - 1
    return scratch + [
        pltpu.SemaphoreType.DMA((len(ones), arrivals)),
        pltpu.SemaphoreType.DMA((len(ones), arrivals)),
    ]


def at_stage(stage, stages, act):
    count = pl.num_programs(0)
    pl.when(pl.program_id(0) == stage * count // stages)(act)


def weights_kernel(in_proj, small, hid, proj_o, small_o, halo_o, halo_buf, halo_sem, local_sem, send_sem, recv_sem):
    me = Place()
    greet(me.around() + [me.along(1), me.along(-1)])
    last = hid.at[pl.ds(hid.shape[0] - HALO, HALO)]
    halo = remote(last, halo_buf, halo_sem.at[0], halo_sem.at[1], me.along(1))
    halo.start()
    gather = Gather(me, [in_proj, small], [proj_o, small_o], local_sem, send_sem, recv_sem)
    for stage in range(4):
        gather.run(stage)
    gather.finish()
    halo.wait()
    halo_o[...] = jnp.where(me.seq > 0, halo_buf[...].astype(F32), 0.0).astype(LOW)


def project_kernel(
    sizes, info, hid, halo, proj, gain, rows, a_log, dt_bias, out_proj,
    normed_o, normed_halo_o, pre_o, maps_o, scaled_o, mixed_o, tail_o, step_o, run_o, run_t_o, sig_o,
    state_o, carry_o, final_o, through_o, out_all,
    ext, state, through, local_sem, send_sem, recv_sem,
):
    inner_width, channels, heads = sizes
    state_size = (channels - inner_width) // 2
    at = pl.program_id(0)
    me = Place()
    gather = Gather(me, [out_proj], [out_all], local_sem, send_sem, recv_sem)

    @pl.when(at == 0)
    def _():
        greet(me.around())

    for stage in range(4):
        at_stage(stage, 4, functools.partial(gather.run, stage))

    gain_row = gain[...]
    taps, offset = rows[0:4], rows[4:5]

    def norm(v):
        v = v.astype(F32)
        return (v * rms_rate(v) * gain_row).astype(LOW)

    weight = proj[:, inner_width : inner_width + channels]

    @pl.when(at == 0)
    def _():
        before = norm(halo[...])
        normed_halo_o[...] = before
        ext[0:EDGE] = nn(before, weight)[HALO - EDGE :]
        state[...] = jnp.zeros_like(state)
        through[...] = jnp.ones_like(through)

    labels = Labels(info, at)
    groups = head_groups(heads, inner_width)
    normed = norm(hid[...])
    normed_o[...] = normed
    mixed = nn(normed, weight)
    raw = nn(normed, proj[:, inner_width + channels :])
    ext[EDGE:] = mixed
    tail_o[0] = ext[0:EDGE]
    mixed_o[...] = mixed
    same = labels.same()
    total = offset + taps[3:4] * mixed
    for j in (1, 2, 3):
        total += taps[3 - j : 4 - j] * (same[:, j : j + 1] * ext[EDGE - j : EDGE - j + BLOCK])
    ext[0:EDGE] = mixed[BLOCK - EDGE :]
    pre_o[...] = total
    act = total * sigmoid(total)
    maps = act[:, inner_width:].astype(LOW)
    maps_o[...] = maps
    z = raw + dt_bias[...]
    step = jnp.maximum(z, 0.0) + log1p_of(jnp.exp(-jnp.abs(z)))
    log_decay = step * (-LOG2E * jnp.exp(a_log[...]))
    run = nn(triangle(), log_decay, HIGHEST)
    step_o[...] = step
    run_o[...] = run
    sig_o[...] = sigmoid(z)
    wide = jnp.concatenate([run, jnp.zeros((BLOCK, 128 - heads), F32)], axis=1)
    run_t_o[0] = jnp.transpose(wide)[:heads]
    last = run[BLOCK - 1 :]
    tail = labels.keep() * jnp.exp2(last - run)
    scaled = spread(step, groups) * act[:, :inner_width]
    scaled_o[...] = scaled.astype(LOW)
    weighted = (spread(tail, groups) * scaled).astype(LOW)
    fresh = tn(maps[:, :state_size], weighted)
    state_o[0] = fresh
    factor = labels.flag()[:, :heads] * jnp.exp2(jnp.broadcast_to(last, (8, heads)))
    through[:, :heads] = through[:, :heads] * factor
    factor = spread(factor, groups)
    carry_o[0] = factor
    state[...] = factor[0:1] * state[...] + fresh

    @pl.when(at == pl.num_programs(0) - 1)
    def _():
        final_o[...] = state[...].astype(LOW)
        through_o[...] = through[...]
        gather.finish()


def inner_kernel(
    sizes, info, normed, proj, maps, scaled, run, run_t, final, through, gate_o, inner_o, inbound_o, *scratch
):
    inner_width, channels, heads = sizes
    state_size = (channels - inner_width) // 2
    head_size = inner_width // heads
    at = pl.program_id(0)
    exchange = Exchange(False, lambda: head_groups(heads, inner_width), final, through, inbound_o, *scratch)
    pl.when(at == 0)(exchange.start)
    pl.when(at == pl.num_programs(0) // 2)(exchange.middle)
    labels = Labels(info, at)
    gate_o[...] = nn(normed[...], proj[...])
    in_map = maps[:, :state_size]
    out_map = maps[:, state_size:]
    q_at = lax.broadcasted_iota(jnp.int32, (BLOCK, BLOCK), 0)
    s_at = lax.broadcasted_iota(jnp.int32, (BLOCK, BLOCK), 1)
    inside = (q_at >= s_at) & (labels.column() == labels.row())
    scores = jnp.where(inside, nt(out_map, in_map), 0.0)
    lane = lax.broadcasted_iota(jnp.int32, (BLOCK, 2 * head_size), 1)
    run_q = run[...]
    for pair in range(heads // 2):
        span = slice(pair * 2 * head_size, (pair + 1) * 2 * head_size)
        values = scaled[:, span]
        parts = []
        for h in (2 * pair, 2 * pair + 1):
            decay = jnp.exp2(jnp.minimum(run_q[:, h : h + 1] - run_t[0, h : h + 1], 0.0))
            parts.append(nn((scores * decay).astype(LOW), values))
        inner_o[:, span] = jnp.where(lane < head_size, parts[0], parts[1])
    pl.when(at == pl.num_programs(0) - 1)(exchange.finish)


def gate_kernel(
    sizes, info, hid, cot, gate, inner, pre, maps, run, state, carry, inbound, out_proj, gain, skip,
    block_o, gated_o, masked_o, back_o, enter_back_o, gate_back_o, row_o, out_back_o, enter_o, leaving_o, gain_o, skip_o,
    now, leaving, through,
):
    inner_width, channels, heads = sizes
    state_size = (channels - inner_width) // 2
    at = pl.program_id(0)
    labels = Labels(info, at)
    groups = head_groups(heads, inner_width)

    @pl.when(at == 0)
    def _():
        now[...] = inbound[...].astype(F32)
        leaving[...] = jnp.zeros_like(leaving)
        through[...] = jnp.ones_like(through)
        gain_o[...] = jnp.zeros_like(gain_o)
        skip_o[...] = jnp.zeros_like(skip_o)

    values = pre[...]
    values = values * sigmoid(values)
    out_map = maps[:, state_size:]
    entry = spread(labels.entry() * jnp.exp2(run[...]), groups)
    entering = now[...]
    enter_o[0] = entering
    enter_high, enter_rest = halves(entering)
    scanned = inner[...] + entry * nn(out_map, enter_high)
    factor = carry[0, 0:1]
    now[...] = factor * entering + state[0]
    mixer = scanned + spread(jnp.broadcast_to(skip[...], (8, heads)), groups)[0:1] * values
    g = gate[...]
    sg = sigmoid(g)
    si = g * sg
    gated = mixer * si
    rate = rms_rate(gated)
    unit = gated * rate
    gain_row = gain[...]
    gated_low = (unit * gain_row).astype(LOW)
    gated_o[...] = gated_low
    valid = labels.valid()
    branch = nn(gated_low, out_proj[...])
    block_o[...] = (valid * (hid[...].astype(F32) + branch)).astype(LOW)
    masked = (valid * cot[...].astype(F32)).astype(LOW)
    masked_o[...] = masked
    back = nt(masked, out_proj[...])
    product = back * unit
    gain_o[...] += jnp.sum(product, axis=0, keepdims=True)
    mean = jnp.mean(product * gain_row, axis=-1, keepdims=True)
    gated_back = rate * (back * gain_row - unit * mean)
    mixer_back = gated_back * si
    gate_back_o[...] = (gated_back * mixer * (sg + si * (1.0 - sg))).astype(LOW)
    skip_o[...] += jnp.sum(mixer_back * values, axis=0, keepdims=True)
    back_low = mixer_back.astype(LOW)
    back_o[...] = back_low
    row_o[...] = head_sums(back_low.astype(F32) * scanned, groups)
    back_high, back_rest = halves(entry * mixer_back)
    enter_back_o[...] = back_high
    out_back_o[...] = nt(back_high, enter_high) + nt(back_rest, enter_high) + nt(back_high, enter_rest)
    leaving[...] += through[0:1] * tn(out_map, back_high)
    through[...] = through[...] * factor

    @pl.when(at == pl.num_programs(0) - 1)
    def _():
        leaving_o[...] = leaving[...].astype(LOW)


def inner_back_kernel(
    sizes, info, maps, scaled, back, run, run_t, gated, masked, normed, gate_back, leaving, through,
    values_o, maps_o, col_o, out_grad_o, gate_grad_o, onward_o, *scratch
):
    inner_width, channels, heads = sizes
    state_size = (channels - inner_width) // 2
    head_size = inner_width // heads
    at = pl.program_id(0)
    exchange = Exchange(True, lambda: head_groups(heads, inner_width), leaving, through, onward_o, *scratch)
    pl.when(at == 0)(exchange.start)
    pl.when(at == pl.num_programs(0) // 2)(exchange.middle)
    out_grad_o[...] = tn(gated[...], masked[...]).astype(LOW)
    gate_grad_o[...] = tn(normed[...], gate_back[...]).astype(LOW)
    labels = Labels(info, at)
    in_map = maps[:, :state_size]
    out_map = maps[:, state_size:]
    s_at = lax.broadcasted_iota(jnp.int32, (BLOCK, BLOCK), 0)
    q_at = lax.broadcasted_iota(jnp.int32, (BLOCK, BLOCK), 1)
    inside = (q_at >= s_at) & (labels.column() == labels.row())
    scores = jnp.where(inside, nt(in_map, out_map), 0.0)
    lane = lax.broadcasted_iota(jnp.int32, (BLOCK, 2 * head_size), 1)
    run_s = run[...]
    total = jnp.zeros((BLOCK, BLOCK), F32)
    for pair in range(heads // 2):
        span = slice(pair * 2 * head_size, (pair + 1) * 2 * head_size)
        values = scaled[:, span]
        grad = back[:, span]
        parts = []
        for h in (2 * pair, 2 * pair + 1):
            mine = (lane < head_size) == (h % 2 == 0)
            decay = jnp.exp2(jnp.minimum(run_t[0, h : h + 1] - run_s[:, h : h + 1], 0.0))
            parts.append(nn((scores * decay).astype(LOW), grad))
            total += decay * nt(jnp.where(mine, values, jnp.zeros_like(values)), grad)
        values_o[:, span] = jnp.where(lane < head_size, parts[0], parts[1])
    total = jnp.where(inside, total, 0.0).astype(LOW)
    maps_o[:, :state_size] = nn(total, out_map)
    maps_o[:, state_size:] = tn(total, in_map)
    col_o[...] = head_sums(values_o[...] * scaled[...].astype(F32), head_groups(heads, inner_width))
    pl.when(at == pl.num_programs(0) - 1)(exchange.finish)


def finish_kernel(
    sizes, info, hid, halo, masked, pre, maps, scaled, back, enter_back, values_in, maps_in, out_in, col_in, row_in,
    step, run, sig, gate_back, enter, carry, onward, mixed, mixed_tail, proj, gain, rows, a_log, skip, inner_gain_sum,
    skip_sum, out_grad, gate_grad,
    late_o, late_halo_o, hid_o, last_o, halo_hid_o, sums_o, out_sum_o, gate_sum_o,
    state, ext, near, local_sem, *scratch
):
    inner_width, channels, heads = sizes
    state_size = (channels - inner_width) // 2
    at = pl.num_programs(0) - 1 - pl.program_id(0)
    first_step = pl.program_id(0) == 0
    last_step = pl.program_id(0) == pl.num_programs(0) - 1

    me = Place()
    grads = [out_grad, gate_grad]
    bufs = [scratch[SCATTER_BUFFERS * a : SCATTER_BUFFERS * (a + 1)] for a in range(2)]

    def part(a, x, core):
        return grads[a].at[pl.ds((x * CORES + core) * me.seqs, me.seqs)]

    scatter = Scatter(
        me, [functools.partial(part, a, core=1 - me.core) for a in range(2)], bufs, *scratch[2 * SCATTER_BUFFERS :]
    )

    def own(a, x):
        return pltpu.make_async_copy(part(a, x, me.core), bufs[a][1].at[x], local_sem.at[a, x])

    def stage_0():
        greet(me.around())
        for a in range(2):
            scatter.send(a, 0)
            for x in range(me.sx):
                own(a, x).start()

    def stage_1():
        for a in range(2):
            for x in range(me.sx):
                own(a, x).wait()
            scatter.absorb(a, 0)
            scatter.send(a, 1)

    def stage_2():
        for a in range(2):
            scatter.absorb(a, 1)
            scatter.send(a, 2)

    def stage_3():
        for a in range(2):
            scatter.absorb(a, 2)
            scatter.send(a, 3)

    for stage, act in enumerate((stage_0, stage_1, stage_2, stage_3)):
        at_stage(stage, 4, act)

    @pl.when(first_step)
    def _():
        state[...] = onward[...].astype(F32)
        ext[0:EDGE] = jnp.zeros((EDGE, channels), F32)
        ext[EDGE + BLOCK :] = jnp.zeros((EDGE, channels), F32)
        sums_o[...] = jnp.zeros_like(sums_o)

    labels = Labels(info, at)
    group = head_groups(heads, inner_width)
    taps = rows[0:4]
    u = pre[...]
    sg = sigmoid(u)
    act = u * sg
    slope = sg + act * (1.0 - sg)
    values = act[:, :inner_width]
    in_map = maps[:, :state_size]
    out_map = maps[:, state_size:]
    run_q = run[...]
    steps = step[...]
    tail = spread(labels.keep() * jnp.exp2(run_q[BLOCK - 1 :] - run_q), group)
    grad = back[...].astype(F32)
    scaled_f = scaled[...].astype(F32)
    state_low = state[...].astype(LOW)
    from_tail = tail * nn(in_map, state_low)
    col_tail = head_sums(scaled_f * from_tail, group)
    scaled_back = values_in[...] + from_tail
    step_back = head_sums(values * scaled_back, group)
    skip_row = spread(jnp.broadcast_to(skip[...], (8, heads)), group)[0:1]
    values_back = spread(steps, group) * scaled_back + skip_row * grad
    in_back = maps_in[:, :state_size] + nt((tail * scaled_f).astype(LOW), state_low)
    out_back = maps_in[:, state_size:] + out_in[...]
    factor = carry[0, 0:1]
    shared = jnp.sum(enter[0] * state[...], axis=0, keepdims=True) * factor
    shared = head_sums(jnp.broadcast_to(shared, (8, inner_width)), group)[0:1]
    state[...] = factor * state[...] + tn(out_map, enter_back[...])
    order = triangle()
    decay_back = (
        tn(order, row_in[...] - col_in[...], HIGHEST) + nn(order, col_tail, HIGHEST) - col_tail + shared
    )
    rate_row = jnp.exp(a_log[...])
    sums_o[7:8, 0:heads] += jnp.sum(decay_back * steps, axis=0, keepdims=True) * -rate_row
    raw_back = (step_back - rate_row * decay_back) * sig[...]
    sums_o[7:8, 128 : 128 + heads] += jnp.sum(raw_back, axis=0, keepdims=True)
    raw_low = raw_back.astype(LOW)
    late_o[:, channels:] = raw_low
    ext[EDGE : EDGE + BLOCK, :inner_width] = values_back * slope[:, :inner_width]
    ext[EDGE : EDGE + BLOCK, inner_width : inner_width + state_size] = (
        in_back * slope[:, inner_width : inner_width + state_size]
    )
    ext[EDGE : EDGE + BLOCK, inner_width + state_size :] = out_back * slope[:, inner_width + state_size :]
    pre_back = ext[EDGE : EDGE + BLOCK]
    near[0:EDGE] = mixed_tail[0]
    near[EDGE:] = mixed[...]
    sums_o[4:5] += jnp.sum(pre_back, axis=0, keepdims=True)
    sums_o[3:4] += jnp.sum(pre_back * near[EDGE:], axis=0, keepdims=True)
    total = taps[3:4] * pre_back
    same = Labels(info, at, BLOCK + EDGE).same()
    for j in (1, 2, 3):
        sums_o[3 - j : 4 - j] += jnp.sum(
            pre_back * (same[:BLOCK, j : j + 1] * near[EDGE - j : EDGE - j + BLOCK]), axis=0, keepdims=True
        )
        total += taps[3 - j : 4 - j] * (same[j : j + BLOCK, j : j + 1] * ext[EDGE + j : EDGE + j + BLOCK])
    mixed_low = total.astype(LOW)
    late_o[:, :channels] = mixed_low
    ext[EDGE + BLOCK :] = ext[EDGE : 2 * EDGE]
    gain_row = gain[...]
    weight = proj[:, inner_width : inner_width + channels]

    def norm_back(normed_back, v):
        rate = rms_rate(v)
        unit = v * rate
        product = normed_back * unit
        mean = jnp.mean(product * gain_row, axis=-1, keepdims=True)
        sums_o[6:7, : v.shape[1]] += jnp.sum(product, axis=0, keepdims=True)
        return rate * (normed_back * gain_row - unit * mean)

    normed_back = (
        nt(gate_back[...], proj[:, :inner_width])
        + nt(mixed_low, weight)
        + nt(raw_low, proj[:, inner_width + channels :])
    )
    result = masked[...].astype(F32) + norm_back(normed_back, hid[...].astype(F32))
    hid_o[...] = result.astype(LOW)

    @pl.when(first_step)
    def _():
        last_o[...] = result[BLOCK - HALO :]

    @pl.when(last_step)
    def _():
        padded = jnp.concatenate([jnp.zeros((EDGE, 8), F32), same[:EDGE]], axis=0)
        edge = jnp.zeros((EDGE, channels), F32)
        for j in (1, 2, 3):
            edge += taps[3 - j : 4 - j] * (padded[j : j + EDGE, j : j + 1] * ext[j : j + EDGE])
        edge_low = jnp.concatenate([jnp.zeros((HALO - EDGE, channels), F32), edge], axis=0).astype(LOW)
        late_halo_o[:, :channels] = edge_low
        late_halo_o[:, channels:] = jnp.zeros((HALO, heads), LOW)
        halo_hid_o[...] = norm_back(nt(edge_low, weight), halo[...].astype(F32))
        sums_o[5:6, :inner_width] = inner_gain_sum[...]
        skip_total = head_sums(jnp.broadcast_to(skip_sum[...], (8, inner_width)), group)
        sums_o[7:8, 256 : 256 + heads] = skip_total[0:1]
        for a, out in enumerate((out_sum_o, gate_sum_o)):
            out[...] = scatter.result(a)
        scatter.settle()


def last_kernel(
    sizes, normed, normed_halo, late, late_halo, gate_sum, sums, halo_hid, last,
    proj_o, taps_o, offset_o, inner_gain_o, gain_o, a_log_o, dt_bias_o, skip_o, last_o,
    halo_buf, halo_sem, small_buf, small_sem, other, *scratch
):
    inner_width, channels, heads = sizes
    me = Place()
    bufs = scratch[:SCATTER_BUFFERS]
    scatter = Scatter(me, [lambda x: other.at[x]], [bufs], *scratch[SCATTER_BUFFERS:])
    greet(me.around() + [me.along(1), me.along(-1)])
    halo = remote(halo_hid, halo_buf, halo_sem.at[0], halo_sem.at[1], me.along(-1))
    halo.start()

    axes = [
        (CORES, me.core, [(1, 1 - me.core, me.twin)]),
        (me.sx, me.x, [(k, p, me.device(x=p)) for k, p in me.peers("x")]),
        (me.sy, me.y, [(k, p, me.device(y=p)) for k, p in me.peers("y")]),
        (me.sz, me.z, [(k, p, me.device(z=p)) for k, p in me.peers("z")]),
    ]

    def small_copies(stage):
        _, mine, peers = axes[stage]
        buf = small_buf.at[stage, mine]
        return [remote(buf, buf, small_sem.at[0, stage, k], small_sem.at[1, stage, mine], device) for k, _, device in peers]

    def small_send(stage, value):
        small_buf[stage, axes[stage][1]] = value
        for copy in small_copies(stage):
            copy.start()

    def small_take(stage):
        size, _, peers = axes[stage]
        for _, p, _ in peers:
            buf = small_buf.at[stage, p]
            remote(buf, buf, small_sem.at[0, stage, 0], small_sem.at[1, stage, p], me.twin).wait_recv()
        total = small_buf[stage, 0]
        for i in range(1, size):
            total = total + small_buf[stage, i]
        return total

    small_send(0, sums[...])

    own_rows = normed.shape[1] // me.count
    half = me.seqs * own_rows
    mine = bufs[1]
    starts = scatter.copies(0, 0)
    for x in range(me.sx):
        span = slice(2 * half * x, 2 * half * (x + 1))
        grad = tn(normed[:, span], late[...]) + tn(normed_halo[:, span], late_halo[...])
        first = me.core == 0
        here = jnp.where(first, grad[:half], grad[half:])
        there = jnp.where(first, grad[half:], grad[:half])
        for i in range(me.seqs):
            other[x, i] = there[i * own_rows : (i + 1) * own_rows].astype(LOW)
            mine[x, i] = here[i * own_rows : (i + 1) * own_rows].astype(LOW)
        for k in range(me.sx):
            pl.when(scatter.order[k] == x)(starts[k].start)
    value = small_take(0)
    small_send(1, value)
    scatter.absorb(0, 0)
    scatter.send(0, 1)
    value = small_take(1)
    small_send(2, value)
    scatter.absorb(0, 1)
    scatter.send(0, 2)
    value = small_take(2)
    small_send(3, value)
    scatter.absorb(0, 2)
    scatter.send(0, 3)
    total = small_take(3)
    mine_at = me.row * me.seqs + me.seq

    def own(v, size):
        width = v.shape[1]
        return pltpu.roll(v, lax.rem(width - mine_at * size, width), 1)[:, :size]

    taps_o[...] = own(total, taps_o.shape[1])[0:4]
    offset_o[...] = own(total, offset_o.shape[1])[4:5]
    inner_gain_o[...] = own(total, inner_gain_o.shape[1])[5:6]
    gain_o[...] = own(total, gain_o.shape[1])[6:7]
    a_log_o[...] = total[7:8, 0:heads]
    dt_bias_o[...] = total[7:8, 128 : 128 + heads]
    skip_o[...] = total[7:8, 256 : 256 + heads]
    halo.wait()
    last_o[...] = last[...] + jnp.where(me.seq < me.seqs - 1, halo_buf[...], 0.0)
    proj_o[:, :inner_width] = gate_sum[...]
    proj_o[:, inner_width:] = scatter.result(0)
    scatter.settle()
    for stage in range(4):
        for copy in small_copies(stage):
            copy.wait_send()


def struct(shape, dtype=F32):
    return jax.ShapeDtypeStruct(shape, dtype)


def run_kernel(kernel, name, count, ins, outs, scratch=(), flip=False, collective_id=None):
    def block(i):
        return count - 1 - i if flip else i

    def spec(array, kind):
        shape = array.shape
        zeros = (0,) * (len(shape) - 1)
        if kind == "any":
            return pl.BlockSpec(memory_space=pl.ANY)
        if kind == "scalar":
            return pl.BlockSpec(memory_space=pltpu.SMEM)
        if kind == "w":
            return pl.BlockSpec(shape, lambda i: (0,) + zeros)
        if kind == "once":
            return pl.BlockSpec(shape, lambda i: (0,) + zeros, pipeline_mode=pl.Buffered(1))
        if kind == "r":
            return pl.BlockSpec((BLOCK,) + shape[1:], lambda i: (block(i),) + zeros)
        if kind == "b":
            return pl.BlockSpec((1,) + shape[1:], lambda i: (block(i),) + zeros)
        if kind == "c":
            return pl.BlockSpec((shape[0], shape[1] // count), lambda i: (0, i))
        if kind == "part":
            return pl.BlockSpec((shape[0] // count, shape[1]), lambda i: (i, 0))
        if kind[0] == "r":
            return pl.BlockSpec((BLOCK, kind[1]), lambda i: (block(i), 0))
        return pl.BlockSpec(kind, lambda i: (0,) * len(kind))

    return pl.pallas_call(
        kernel,
        name=name,
        grid=(count,),
        in_specs=[spec(a, k) for a, k in ins],
        out_specs=[spec(a, k) for a, k in outs],
        out_shape=[a for a, _ in outs],
        scratch_shapes=list(scratch),
        compiler_params=pltpu.CompilerParams(
            dimension_semantics=("arbitrary",),
            vmem_limit_bytes=VMEM_BYTES,
            collective_id=collective_id,
            has_side_effects=collective_id is not None,
        ),
    )(*[a for a, _ in ins])


def body(
    hidden, lengths, cotangent, norm_gain, in_proj, conv_weight, conv_bias, a_log, dt_bias, skip_weight, inner_gain,
    out_proj,
):
    length, model = hidden.shape[1:]
    count = length // BLOCK
    heads = a_log.shape[0]
    devices = lax.axis_size(AXES)
    seqs = lax.axis_size("seq")
    inner_width = out_proj.shape[0] * devices
    channels = conv_weight.shape[1] * devices
    state_size = (channels - inner_width) // 2
    sizes = (inner_width, channels, heads)
    hid = hidden[0]
    cot = cotangent[0]
    width, part = conv_weight.shape
    own_rows, columns = in_proj.shape
    a_row, bias_row, skip_row = a_log[None], dt_bias[None], skip_weight[None]
    info = jnp.concatenate([lengths, (lax.axis_index("seq") * length).reshape(1, 1)], axis=1)

    def padded(v):
        v = v.astype(F32)
        return jnp.pad(v, ((0, 0), (0, part - v.shape[1])))

    small = jnp.concatenate(
        [conv_weight.astype(F32), padded(conv_bias[None]), padded(inner_gain[None]), padded(norm_gain[None])]
        + [jnp.zeros((8 - width - 3, part), F32)]
    )
    proj_all, small_all, halo = run_kernel(
        weights_kernel, "weights", 1,
        [(in_proj, "any"), (small, "any"), (hid, "any")],
        [
            (struct((devices,) + in_proj.shape, LOW), "any"), (struct((devices,) + small.shape), "any"),
            (struct((HALO, model), LOW), "w"),
        ],
        [pltpu.VMEM((HALO, model), LOW), pltpu.SemaphoreType.DMA((2,))] + gather_semaphores(2),
        collective_id=0,
    )
    proj_full = proj_all.reshape(model, columns)
    rows = jnp.moveaxis(small_all, 1, 0).reshape(8, channels)
    inner_gain_row = small_all[:, width + 1, : inner_gain.shape[0]].reshape(1, inner_width)
    gain_row = small_all[:, width + 2, :own_rows].reshape(1, model)

    token = struct((length, inner_width), LOW)
    (
        normed, normed_halo, pre, maps, scaled, mixed, mixed_tail, step, run, run_t, sig, state, carry, final_state,
        through, out_all,
    ) = run_kernel(
        functools.partial(project_kernel, sizes), "project", count,
        [
            (info, "scalar"), (hid, "r"), (halo, "w"), (proj_full, "once"), (gain_row, "w"), (rows, "w"), (a_row, "w"),
            (bias_row, "w"), (out_proj, "any"),
        ],
        [
            (struct((length, model), LOW), "r"), (struct((HALO, model), LOW), "w"),
            (struct((length, channels)), "r"), (struct((length, 2 * state_size), LOW), "r"),
            (token, "r"), (struct((length, channels)), "r"),
            (struct((count, EDGE, channels)), "b"), (struct((length, heads)), "r"), (struct((length, heads)), "r"),
            (struct((count, heads, BLOCK)), "b"), (struct((length, heads)), "r"),
            (struct((count, state_size, inner_width)), "b"), (struct((count, 8, inner_width)), "b"),
            (struct((state_size, inner_width), LOW), "w"), (struct((8, 128)), "w"),
            (struct((devices,) + out_proj.shape, LOW), "any"),
        ],
        [
            pltpu.VMEM((EDGE + BLOCK, channels), F32), pltpu.VMEM((state_size, inner_width), F32),
            pltpu.VMEM((8, 128), F32),
        ] + gather_semaphores(1),
        collective_id=1,
    )
    out_full = out_all.reshape(inner_width, model)
    pieces = (seqs, state_size // seqs, inner_width)
    gate, inner, inbound = run_kernel(
        functools.partial(inner_kernel, sizes), "inner", count,
        [
            (info, "scalar"), (normed, "r"), (proj_full, (model, inner_width)), (maps, "r"), (scaled, "r"), (run, "r"),
            (run_t, "b"), (final_state.reshape(pieces), "w"), (through, "w"),
        ],
        [
            (struct((length, inner_width)), "r"), (struct((length, inner_width)), "r"), (struct(pieces, LOW), "w"),
        ],
        exchange_scratch(pieces),
        collective_id=2,
    )
    (
        block_out, gated, masked, back, enter_back, gate_back, row_term, out_in, enter, leaving, inner_gain_sum, skip_sum,
    ) = run_kernel(
        functools.partial(gate_kernel, sizes), "gate", count,
        [
            (info, "scalar"), (hid, "r"), (cot, "r"), (gate, "r"), (inner, "r"), (pre, ("r", inner_width)), (maps, "r"),
            (run, "r"), (state, "b"), (carry, "b"), (inbound.reshape(state_size, inner_width), "w"), (out_full, "once"),
            (inner_gain_row, "w"), (skip_row, "w"),
        ],
        [
            (struct((length, model), LOW), "r"), (token, "r"), (struct((length, model), LOW), "r"), (token, "r"),
            (token, "r"), (token, "r"), (struct((length, heads)), "r"), (struct((length, state_size)), "r"),
            (struct((count, state_size, inner_width)), "b"), (struct((state_size, inner_width), LOW), "w"),
            (struct((1, inner_width)), "w"), (struct((1, inner_width)), "w"),
        ],
        [
            pltpu.VMEM((state_size, inner_width), F32), pltpu.VMEM((state_size, inner_width), F32),
            pltpu.VMEM((8, inner_width), F32),
        ],
    )
    values_in, maps_in, col_in, out_grad, gate_grad, onward = run_kernel(
        functools.partial(inner_back_kernel, sizes), "inner_back", count,
        [
            (info, "scalar"), (maps, "r"), (scaled, "r"), (back, "r"), (run, "r"), (run_t, "b"), (gated, "c"),
            (masked, "w"), (normed, "w"), (gate_back, "c"), (leaving.reshape(pieces), "w"), (through, "w"),
        ],
        [
            (struct((length, inner_width)), "r"), (struct((length, 2 * state_size)), "r"),
            (struct((length, heads)), "r"), (struct((inner_width, model), LOW), "part"),
            (struct((model, inner_width), LOW), "c"), (struct(pieces, LOW), "w"),
        ],
        exchange_scratch(pieces),
        collective_id=3,
    )
    gate_one = (own_rows, inner_width)
    late_width = columns - inner_width
    late, late_halo, hid_grad, last_rows, halo_hid, sums, out_sum, gate_sum = run_kernel(
        functools.partial(finish_kernel, sizes), "finish", count,
        [
            (info, "scalar"), (hid, "r"), (halo, "w"), (masked, "r"), (pre, "r"), (maps, "r"), (scaled, "r"),
            (back, "r"), (enter_back, "r"), (values_in, "r"), (maps_in, "r"), (out_in, "r"), (col_in, "r"),
            (row_term, "r"), (step, "r"), (run, "r"), (sig, "r"), (gate_back, "r"), (enter, "b"), (carry, "b"),
            (onward.reshape(state_size, inner_width), "w"), (mixed, "r"), (mixed_tail, "b"), (proj_full, "once"),
            (gain_row, "w"), (rows, "w"), (a_row, "w"), (skip_row, "w"), (inner_gain_sum, "w"), (skip_sum, "w"),
            (out_grad.reshape(devices, -1, model), "any"), (gate_grad.reshape(devices, -1, inner_width), "any"),
        ],
        [
            (struct((length, late_width), LOW), "r"), (struct((HALO, late_width), LOW), "w"),
            (struct((length, model), LOW), "r"), (struct((HALO, model)), "w"), (struct((HALO, model)), "w"),
            (struct((8, channels)), "w"), (struct(out_proj.shape), "w"), (struct(gate_one), "w"),
        ],
        [
            pltpu.VMEM((state_size, inner_width), F32), pltpu.VMEM((2 * EDGE + BLOCK, channels), F32),
            pltpu.VMEM((EDGE + BLOCK, channels), F32), pltpu.SemaphoreType.DMA((2, lax.axis_size("row") // CORES)),
        ] + scatter_scratch([out_proj.shape, gate_one]),
        flip=True,
        collective_id=4,
    )
    late_one = (own_rows, late_width)
    most = max(CORES, lax.axis_size("row") // CORES, DEPTH, seqs // DEPTH)
    sx = lax.axis_size("row") // CORES
    row = struct((1, heads))
    proj_sum, taps_sum, offset_sum, inner_sum, gain_sum, a_log_sum, dt_bias_sum, skip_total, last_rows = run_kernel(
        functools.partial(last_kernel, sizes), "last", 1,
        [
            (normed, "once"), (normed_halo, "w"), (late, "once"), (late_halo, "w"), (gate_sum, "w"), (sums, "w"),
            (halo_hid, "w"), (last_rows, "w"),
        ],
        [
            (struct(in_proj.shape), "w"), (struct((width, part)), "w"), (struct((1, part)), "w"),
            (struct((1, inner_gain.shape[0])), "w"), (struct((1, own_rows)), "w"), (row, "w"), (row, "w"), (row, "w"),
            (struct((HALO, model)), "w"),
        ],
        [
            pltpu.VMEM((HALO, model), F32), pltpu.SemaphoreType.DMA((2,)), pltpu.VMEM((4, most, 8, channels), F32),
            pltpu.SemaphoreType.DMA((2, 4, most)), pltpu.VMEM((sx, seqs) + late_one, LOW),
        ] + scatter_scratch([late_one]),
        collective_id=5,
    )
    hidden_grad = jnp.concatenate([hid_grad[: length - HALO], last_rows.astype(LOW)])
    return (
        block_out[None], hidden_grad[None], gain_sum[0], proj_sum, taps_sum, offset_sum[0], a_log_sum[0], dt_bias_sum[0],
        skip_total[0], inner_sum[0], out_sum,
    )


def solution(mesh):
    weights = P(AXES)
    tokens = P("row", "seq", None)
    rows = P(AXES, None)
    return jax.shard_map(
        body,
        mesh=mesh,
        in_specs=(
            tokens, P("row", None), tokens, weights, rows, P(None, AXES), weights, P(), P(), P(), weights, rows,
        ),
        out_specs=(tokens, tokens, weights, rows, P(None, AXES), weights, P(), P(), P(), weights, rows),
        check_vma=False,
    )
```

```python
import functools

import jax
import jax.numpy as jnp
from jax import lax
from jax.experimental import pallas as pl
from jax.experimental.pallas import tpu as pltpu
from jax.sharding import PartitionSpec as P

BLOCK = 256
EPS = 1e-05
LOG2E = 1.4426950408889634
HIGHEST = lax.Precision.HIGHEST
F32 = jnp.float32
LOW = jnp.bfloat16
EDGE = 8
HALO = 16
AXES = ("row", "seq")
MESH = pl.DeviceIdType.MESH
CORES = 2
DEPTH = 4
VMEM_BYTES = 63 * 1024 * 1024


def nn(a, b, precision=None):
    return lax.dot_general(
        a, b, (((1,), (0,)), ((), ())), precision=precision, preferred_element_type=F32
    )


def nt(a, b):
    return lax.dot_general(a, b, (((1,), (1,)), ((), ())), preferred_element_type=F32)


def tn(a, b, precision=None):
    return lax.dot_general(
        a, b, (((0,), (0,)), ((), ())), precision=precision, preferred_element_type=F32
    )


def halves(v):
    high = v.astype(LOW)
    return high, (v - high.astype(F32)).astype(LOW)


def head_groups(heads, width, copies=1):
    column = lax.broadcasted_iota(jnp.int32, (copies * heads, width), 1)
    first = lax.rem(lax.broadcasted_iota(jnp.int32, (copies * heads, width), 0), heads) * (width // heads)
    return ((column >= first) & (column < first + width // heads)).astype(F32).astype(LOW)


def spread(v, pairs):
    return nn(jnp.concatenate(halves(v), axis=1), pairs)


def head_sums(v, groups):
    high, rest = halves(v)
    return nt(high, groups) + nt(rest, groups)


def row_sums(v, groups):
    wide = jnp.concatenate([jnp.broadcast_to(part, (16, v.shape[1])) for part in halves(v)], axis=0)
    sums = nt(wide, groups)
    return sums[0:1] + sums[16:17]


def triangle():
    return (
        lax.broadcasted_iota(jnp.int32, (BLOCK, BLOCK), 0) >= lax.broadcasted_iota(jnp.int32, (BLOCK, BLOCK), 1)
    ).astype(F32)


def sigmoid(v):
    return 0.5 + 0.5 * jnp.tanh(0.5 * v)


def silu(v):
    half = 0.5 * v
    return half + half * jnp.tanh(half)


def silu_parts(v):
    half = 0.5 * v
    curve = jnp.tanh(half)
    value = half + half * curve
    rate = 0.5 + 0.5 * curve
    return value, rate + value - value * rate


def log1p_of(v):
    series = v * (1.0 - v * (0.5 - v * (1.0 / 3.0 - 0.25 * v)))
    return jnp.where(v < 0.01, series, jnp.log(1.0 + v))


def rms_rate(v):
    return lax.rsqrt(jnp.mean(v * v, axis=-1, keepdims=True) + EPS)


class Labels:
    def __init__(self, info, block, rows=BLOCK):
        slots = info.shape[1] - 1
        self.ends, total = [], 0
        for i in range(slots):
            total = total + info[0, i]
            self.ends.append(total)
        self.base = info[0, slots] + block * BLOCK
        self.rows = rows

    def of(self, place):
        total = sum((place >= end).astype(jnp.int32) for end in self.ends)
        return jnp.where(place < 0, -1, total)

    def column(self):
        return self.of(self.base + lax.broadcasted_iota(jnp.int32, (self.rows, 1), 0))

    def row(self):
        return self.of(self.base + lax.broadcasted_iota(jnp.int32, (1, self.rows), 1))

    def before(self):
        return self.of(self.base - 1)

    def last(self):
        return self.of(self.base + BLOCK - 1)

    def entry(self):
        return (self.column() == self.before()).astype(F32)

    def keep(self):
        return (self.column() == self.last()).astype(F32)

    def flag(self):
        return (jnp.full((8, 128), self.before(), jnp.int32) == self.last()).astype(F32)

    def valid(self):
        place = self.base + lax.broadcasted_iota(jnp.int32, (self.rows, 1), 0)
        return (place < self.ends[-1]).astype(F32)

    def same(self):
        shape = (self.rows, 8)
        place = self.base + lax.broadcasted_iota(jnp.int32, shape, 0)
        own = self.of(place)
        return (self.of(place - lax.broadcasted_iota(jnp.int32, shape, 1)) == own).astype(F32)


class Place:
    def __init__(self):
        rows, self.seqs = lax.axis_size("row"), lax.axis_size("seq")
        self.sx, self.sz = rows // CORES, DEPTH
        self.sy = self.seqs // DEPTH
        row, seq = lax.axis_index("row"), lax.axis_index("seq")
        self.x, self.core = lax.div(row, CORES), lax.rem(row, CORES)
        self.z, self.y = lax.div(seq, self.sy), lax.rem(seq, self.sy)
        self.row, self.seq = row, seq
        self.count = rows * self.seqs
        self.twin = self.device(core=1 - self.core)

    def device(self, x=None, core=None, z=None, y=None):
        x = self.x if x is None else x
        core = self.core if core is None else core
        z = self.z if z is None else z
        y = self.y if y is None else y
        return {"row": x * CORES + core, "seq": z * self.sy + y}

    def slot(self, x=None, core=None, z=None, y=None):
        at = self.device(x, core, z, y)
        return at["row"] * self.seqs + at["seq"]

    def peers(self, axis):
        size, mine = {"x": (self.sx, self.x), "y": (self.sy, self.y), "z": (self.sz, self.z)}[axis]
        return [(k, lax.rem(mine + k, size)) for k in range(1, size)]

    def around(self):
        return (
            [self.device(x=p) for _, p in self.peers("x")]
            + [self.device(y=p) for _, p in self.peers("y")]
            + [self.device(z=p) for _, p in self.peers("z")]
            + [self.twin]
        )

    def along(self, by):
        return {"seq": lax.rem(self.seq + by + self.seqs, self.seqs)}


def greet(devices):
    barrier = pltpu.get_barrier_semaphore()
    for device in devices:
        pl.semaphore_signal(barrier, inc=1, device_id=device, device_id_type=MESH)
    pl.semaphore_wait(barrier, len(devices))


def remote(source, target, send_sem, recv_sem, device):
    return pltpu.make_async_remote_copy(
        src_ref=source, dst_ref=target, send_sem=send_sem, recv_sem=recv_sem, device_id=device, device_id_type=MESH
    )


def guarded(act, when):
    if when is None:
        act()
    else:
        pl.when(when)(act)


class Gather:
    def __init__(self, me, ins, outs, local_sem, send_sem, recv_sem):
        self.me, self.ins, self.outs = me, ins, outs
        self.local_sem, self.send_sem, self.recv_sem = local_sem, send_sem, recv_sem
        self.steps = [self.plan(point) for point in range(7)]

    def plan(self, point):
        me = self.me
        xs = [p for _, p in me.peers("x")]
        ys = [p for _, p in me.peers("y")]
        above, below = me.z + 1 < me.sz, me.z > 0
        up, down = (me.device(z=me.z + 1), above), (me.device(z=me.z - 1), below)
        around = [(me.device(y=p), None) for p in ys] + [(me.device(x=p), None) for p in xs] + [(me.twin, None)]
        if point == 0:
            return [(None, None, [up, down] + around)]
        if point < me.sz:
            found = []
            for z, comes, on in ((me.z - point, me.z >= point, up), (me.z + point, me.z + point < me.sz, down)):
                on = (on[0], jnp.logical_and(comes, on[1]))
                found.append((me.slot(z=z), comes, [on] + [(device, comes) for device, _ in around]))
            return found
        found = []
        turns = [lax.rem(me.z + k, me.sz) for k in range(me.sz)]
        first, last = {4: (0, 2), 5: (2, 4), 6: (0, 4)}[point]
        for z in turns[first:last]:
            even = lax.rem(z, 2) == 0
            if point < 6:
                for y in ys:
                    found.append((me.slot(z=z, y=y), None, [(me.device(x=p), even) for p in xs] + [(me.twin, None)]))
                for x in xs:
                    to = [(me.device(y=p), jnp.logical_not(even)) for p in ys] + [(me.twin, None)]
                    found.append((me.slot(z=z, x=x), None, to))
            else:
                for y in ys:
                    for x in xs:
                        found.append((me.slot(z=z, x=x, y=y), None, [(me.twin, None)]))
        return found

    def copies(self, a, point):
        index = sum(len(to) for earlier in self.steps[:point] for _, _, to in earlier)
        found = []
        for slot, comes, to in self.steps[point]:
            at = self.me.slot() if slot is None else slot
            source = self.ins[a] if slot is None else self.outs[a].at[at]
            group = []
            for device, when in to:
                group.append(
                    (remote(source, self.outs[a].at[at], self.send_sem.at[a, index], self.recv_sem.at[a, at], device), when)
                )
                index += 1
            found.append((slot, comes, group))
        return found

    def arrived(self, a, slot, comes=None):
        block = self.outs[a].at[slot]
        guarded(remote(block, block, self.send_sem.at[a, 0], self.recv_sem.at[a, slot], self.me.twin).wait_recv, comes)

    def own(self, a):
        return pltpu.make_async_copy(self.ins[a], self.outs[a].at[self.me.slot()], self.local_sem.at[a])

    def run(self, point):
        for a in range(len(self.ins)):
            if point == 0:
                self.own(a).start()
            for slot, comes, group in self.copies(a, point):
                if slot is not None:
                    self.arrived(a, slot, comes)
                for copy, when in group:
                    guarded(copy.start, when)

    def finish(self, a):
        me = self.me
        for x in range(me.sx):
            for seq in range(me.seqs):
                self.arrived(a, (x * CORES + 1 - me.core) * me.seqs + seq)
        self.own(a).wait()

    def settle(self):
        for a in range(len(self.ins)):
            for point in range(7):
                for _, _, group in self.copies(a, point):
                    for copy, when in group:
                        guarded(copy.wait_send, when)


def gather_semaphores(arrays):
    devices = lax.axis_size(AXES)
    return [
        pltpu.SemaphoreType.DMA((arrays,)),
        pltpu.SemaphoreType.DMA((arrays, 4 * devices)),
        pltpu.SemaphoreType.DMA((arrays, devices)),
    ]


class Exchange:
    def __init__(self, reverse, group, state, through, landed, out, parts, factors, ready, sems):
        self.reverse, self.group = reverse, group
        self.state, self.through, self.landed, self.out = state, through, landed, out
        self.parts, self.factors, self.ready, self.sems = parts, factors, ready, sems
        self.size, self.mine = lax.axis_size("seq"), lax.axis_index("seq")

    def copy(self, source, target, kind, index_out, index_in, peer):
        return remote(source, target, self.sems.at[kind, index_out], self.sems.at[kind + 1, index_in], {"seq": peer})

    def first(self):
        found = []
        for k in range(1, self.size):
            peer = lax.rem(self.mine + k, self.size)
            found.append(self.copy(self.through, self.factors.at[self.mine], 2, k, self.mine, peer))
            found.append(self.copy(self.state.at[peer], self.parts.at[self.mine], 0, k, self.mine, peer))
        return found

    def result(self, j):
        return self.copy(self.ready.at[j], self.out.at[self.mine], 4, j, self.mine, j)

    def start(self):
        greet([{"seq": lax.rem(self.mine + k, self.size)} for k in range(1, self.size)])
        for copy in self.first():
            copy.start()
        self.parts[self.mine] = self.state[self.mine]
        self.factors[self.mine] = self.through[...]

    def middle(self):
        group = self.group()
        heads = group.shape[0] // 2
        total = jnp.zeros(self.state.shape[1:], F32)
        for k in range(self.size):
            j = self.size - 1 - k if self.reverse else k
            self.ready[j] = total.astype(LOW)

            @pl.when(self.mine != j)
            def _(j=j):
                self.result(j).start()
                self.copy(self.through, self.factors.at[j], 2, 0, j, j).wait_recv()
                self.copy(self.state.at[0], self.parts.at[j], 0, 0, j, j).wait_recv()

            factor = spread(self.factors[j][:, :heads], group)
            total = factor[0:1] * total + self.parts[j].astype(F32)
        self.out[self.mine] = self.ready[self.mine]

    def finish(self):
        for k in range(1, self.size):
            j = lax.rem(self.mine + k, self.size)
            self.copy(self.ready.at[j], self.out.at[j], 4, j, j, j).wait_recv()
        self.landed[...] = self.out[...]
        for copy in self.first():
            copy.wait_send()
        for j in range(self.size):
            pl.when(self.mine != j)(self.result(j).wait_send)


def exchange_scratch(pieces):
    size = pieces[0]
    return [
        pltpu.VMEM(pieces, LOW), pltpu.VMEM(pieces, LOW), pltpu.VMEM((size, 8, 128), F32), pltpu.VMEM(pieces, LOW),
        pltpu.SemaphoreType.DMA((6, size)),
    ]


def add_slots(target, first, source, start, pieces):
    def step(i, _):
        at = first + i
        target[at] = (target[at].astype(F32) + source[start + i].astype(F32)).astype(target.dtype)
        return 0

    lax.fori_loop(0, pieces, step, 0)


class Scatter:
    def __init__(self, me, sources, bufs, send_sem, recv_sem):
        self.me, self.sources, self.bufs = me, sources, bufs
        self.send_sem, self.recv_sem = send_sem, recv_sem
        self.groups = [(k, lax.rem(me.z + k, me.sz)) for k in list(range(1, me.sz)) + [0]]

    def plan(self, a, stage, group):
        me = self.me
        sx, sy = me.sx, me.sy
        twin_buf, total, from_x, from_y, from_y2, from_x2, from_z = self.bufs[a]
        xs, ys = me.peers("x"), me.peers("y")
        k, z = self.groups[group]
        along_x = k % 2 == 0
        if stage == 0:
            return [
                (self.sources[a](x, z * sy, sy), twin_buf.at[x, pl.ds(z * sy, sy)], x, me.twin) for x in range(sx)
            ]
        if stage == 1 and along_x:
            return [
                (total.at[x, pl.ds(z * sy, sy)], from_x.at[i - 1, k], sx + i - 1, me.device(x=x)) for i, x in xs
            ]
        if stage == 1:
            return [
                (total.at[x, z * sy + y], from_y.at[i - 1, k, x], sx + (i - 1) * sx + x, me.device(y=y))
                for i, y in ys
                for x in range(sx)
            ]
        start = sx + max(sx - 1, (sy - 1) * sx)
        if stage == 2 and along_x:
            return [
                (total.at[me.x, z * sy + y], from_y2.at[i - 1, k], start + i - 1, me.device(y=y)) for i, y in ys
            ]
        if stage == 2:
            return [
                (total.at[x, z * sy + me.y], from_x2.at[i - 1, k], start + i - 1, me.device(x=x)) for i, x in xs
            ]
        if k == 0:
            return []
        start += max(sx - 1, sy - 1)
        return [(total.at[me.x, z * sy + me.y], from_z.at[k - 1], start, me.device(z=z))]

    def copies(self, a, stage, group, only=None):
        k = self.groups[group][0]
        return [
            remote(source, target, self.send_sem.at[a, k, number], self.recv_sem.at[a, k, number], device)
            for source, target, number, device in self.plan(a, stage, group)
            if only is None or number == only
        ]

    def send(self, stage, groups):
        for a in range(len(self.sources)):
            for group in groups:
                for copy in self.copies(a, stage, group):
                    copy.start()

    def absorb(self, stage, groups):
        me = self.me
        sy = me.sy
        for a in range(len(self.sources)):
            twin_buf, total, from_x, from_y, from_y2, from_x2, from_z = self.bufs[a]
            for group in groups:
                k, z = self.groups[group]
                for copy in self.copies(a, stage, group):
                    copy.wait_recv()
                if stage == 0:
                    for x in range(me.sx):
                        add_slots(total.at[x], z * sy, twin_buf.at[x], z * sy, sy)
                elif stage == 1 and k % 2 == 0:
                    for i in range(me.sx - 1):
                        add_slots(total.at[me.x], z * sy, from_x.at[i, k], 0, sy)
                elif stage == 1:
                    for i in range(sy - 1):
                        for x in range(me.sx):
                            add_slots(total.at[x], z * sy + me.y, from_y.at[i, k], x, 1)
                else:
                    source = from_y2 if k % 2 == 0 else from_x2
                    for i in range((sy if k % 2 == 0 else me.sx) - 1):
                        add_slots(total.at[me.x], z * sy + me.y, source.at[i], k, 1)
                for copy in self.copies(a, stage + 1, group):
                    copy.start()

    def result(self, a):
        me = self.me
        total, from_z = self.bufs[a][1], self.bufs[a][6]
        result = total[me.x, me.z * me.sy + me.y].astype(F32)
        for group, (k, _) in enumerate(self.groups):
            if k:
                for copy in self.copies(a, 3, group):
                    copy.wait_recv()
                result = result + from_z[k - 1].astype(F32)
        return result

    def settle(self):
        for a in range(len(self.sources)):
            for stage in range(4):
                for group in range(len(self.groups)):
                    for copy in self.copies(a, stage, group):
                        copy.wait_send()


SCATTER_BUFFERS = 7


def scatter_scratch(ones, dtype=LOW):
    rows, seqs = lax.axis_size("row"), lax.axis_size("seq")
    sx, sz, sy = rows // CORES, DEPTH, seqs // DEPTH
    scratch = []
    for one in ones:
        for lead in ((sx, seqs), (sx, seqs), (sx - 1, sz, sy), (sy - 1, sz, sx), (sy - 1, sz), (sx - 1, sz), (sz - 1,)):
            scratch.append(pltpu.VMEM(lead + tuple(one), dtype))
    most = sx + max(sx - 1, (sy - 1) * sx) + max(sx - 1, sy - 1) + 1
    return scratch + [pltpu.SemaphoreType.DMA((len(ones), sz, most))] * 2


class Points:
    def __init__(self, acts, hooks, first=0):
        self.acts, self.hooks, self.first = acts, hooks, first

    def hook(self, number):
        count = pl.num_programs(0) - self.first
        for index, act in enumerate(self.acts):
            at = index * self.hooks * count // len(self.acts)
            if at % self.hooks == number:
                pl.when(pl.program_id(0) == self.first + at // self.hooks)(act)


def project_kernel(
    sizes, info, hid, hid_all, a_log, dt_bias, in_proj, out_proj, taps, offset, inner_gain, gain,
    normed_o, normed_halo_o, pre_o, maps_o, scaled_o, mixed_o, tail_o, step_o, run_o, run_t_o, sig_o,
    state_o, carry_o, final_o, through_o, late_o, rows_o, inner_gain_o, gain_o, halo_o, gate_all, out_all,
    ext, state, through, small, small_all, late_all, halo_buf, halo_sem, *sems
):
    inner_width, channels, heads = sizes
    state_size = (channels - inner_width) // 2
    at = pl.program_id(0) - 1
    me = Place()
    width, part = taps.shape
    own_rows = in_proj.shape[0]
    late_part = in_proj.at[:, pl.ds(inner_width, in_proj.shape[1] - inner_width)]
    gate_part = in_proj.at[:, pl.ds(0, inner_width)]
    now = Gather(me, [small, late_part], [small_all, late_all], *sems[:3])
    later = Gather(me, [gate_part, out_proj], [gate_all, out_all], *sems[3:])

    @pl.when(at < 0)
    def _():
        small[...] = jnp.zeros_like(small)
        small[0:width, 0:part] = taps[...].astype(F32)
        for k, piece in enumerate((offset, inner_gain, gain)):
            small[width + k : width + k + 1, 0 : piece.shape[1]] = piece[...].astype(F32)
        greet(me.around() + [me.along(1), me.along(-1)])
        last = hid_all.at[pl.ds(hid_all.shape[0] - HALO, HALO)]
        halo = remote(last, halo_buf, halo_sem.at[0], halo_sem.at[1], me.along(1))
        halo.start()
        for point in range(4):
            now.run(point)
        later.run(0)
        for point in range(4, 7):
            now.run(point)
        later.run(1)
        now.finish(0)
        for d in range(small_all.shape[0]):
            rows_o[0 : width + 1, d * part : (d + 1) * part] = small_all[d, 0 : width + 1, 0:part]
            for k, (out, piece) in enumerate(((inner_gain_o, inner_gain), (gain_o, gain))):
                size = piece.shape[1]
                out[:, d * size : (d + 1) * size] = small_all[d, width + 1 + k : width + 2 + k, 0:size]
        halo.wait()
        halo_o[...] = jnp.where(me.seq > 0, halo_buf[...].astype(F32), 0.0).astype(LOW)
        now.finish(1)
        for d in range(small_all.shape[0]):
            late_o[d * own_rows : (d + 1) * own_rows] = late_all[d]

    @pl.when(at >= 0)
    def _():
        project_step(
            sizes, info, hid, halo_o, late_o, gain_o, rows_o, a_log, dt_bias,
            normed_o, normed_halo_o, pre_o, maps_o, scaled_o, mixed_o, tail_o, step_o, run_o, run_t_o, sig_o,
            state_o, carry_o, final_o, through_o, ext, state, through, at,
            Points([functools.partial(later.run, point) for point in range(2, 7)], 2, 1),
        )

    @pl.when(at == pl.num_programs(0) - 2)
    def _():
        for a in range(2):
            later.finish(a)
        now.settle()
        later.settle()


def project_step(
    sizes, info, hid, halo, late, gain, rows, a_log, dt_bias,
    normed_o, normed_halo_o, pre_o, maps_o, scaled_o, mixed_o, tail_o, step_o, run_o, run_t_o, sig_o,
    state_o, carry_o, final_o, through_o, ext, state, through, at, points,
):
    inner_width, channels, heads = sizes
    state_size = (channels - inner_width) // 2
    points.hook(0)
    gain_row = gain[...]
    taps, offset = rows[0:4], rows[4:5]

    def norm(v):
        v = v.astype(F32)
        return (v * rms_rate(v) * gain_row).astype(LOW)

    weight = late[:, :channels]

    @pl.when(at == 0)
    def _():
        before = norm(halo[...])
        normed_halo_o[...] = before
        ext[0:EDGE] = nn(before, weight)[HALO - EDGE :]
        state[...] = jnp.zeros_like(state)
        through[...] = jnp.ones_like(through)

    labels = Labels(info, at)
    pairs = head_groups(heads, inner_width, 2)
    normed = norm(hid[...])
    normed_o[...] = normed
    mixed = nn(normed, weight)
    raw = nn(normed, late[:, channels:])
    ext[EDGE:] = mixed
    tail_o[0] = ext[0:EDGE]
    mixed_o[...] = mixed
    same = labels.same()
    total = offset + taps[3:4] * mixed
    for j in (1, 2, 3):
        total += taps[3 - j : 4 - j] * (same[:, j : j + 1] * ext[EDGE - j : EDGE - j + BLOCK])
    ext[0:EDGE] = mixed[BLOCK - EDGE :]
    pre_o[...] = total
    points.hook(1)
    act = silu(total)
    maps = act[:, inner_width:].astype(LOW)
    maps_o[...] = maps
    z = raw + dt_bias[...]
    step = jnp.maximum(z, 0.0) + log1p_of(jnp.exp(-jnp.abs(z)))
    log_decay = step * (-LOG2E * jnp.exp(a_log[...]))
    run = nn(triangle(), log_decay, HIGHEST)
    step_o[...] = step
    run_o[...] = run
    sig_o[...] = sigmoid(z)
    wide = jnp.concatenate([run, jnp.zeros((BLOCK, 128 - heads), F32)], axis=1)
    run_t_o[0] = jnp.transpose(wide)[:heads]
    last = run[BLOCK - 1 :]
    tail = labels.keep() * jnp.exp2(last - run)
    scaled = spread(step, pairs) * act[:, :inner_width]
    scaled_o[...] = scaled.astype(LOW)
    weighted = (spread(tail, pairs) * scaled).astype(LOW)
    fresh = tn(maps[:, :state_size], weighted)
    state_o[0] = fresh
    factor = labels.flag()[:, :heads] * jnp.exp2(jnp.broadcast_to(last, (8, heads)))
    through[:, :heads] = through[:, :heads] * factor
    factor = spread(factor, pairs)
    carry_o[0] = factor
    state[...] = factor[0:1] * state[...] + fresh

    @pl.when(at == pl.num_programs(0) - 2)
    def _():
        final_o[...] = state[...].astype(LOW)
        through_o[...] = through[...]


def inner_kernel(
    sizes, info, normed, proj, out_proj, cot, maps, scaled, run, run_t, final, through,
    gate_o, inner_o, masked_o, back_o, inbound_o, *scratch
):
    inner_width, channels, heads = sizes
    state_size = (channels - inner_width) // 2
    head_size = inner_width // heads
    at = pl.program_id(0)
    exchange = Exchange(False, lambda: head_groups(heads, inner_width, 2), final, through, inbound_o, *scratch)
    pl.when(at == 0)(exchange.start)
    pl.when(at == pl.num_programs(0) // 2)(exchange.middle)
    labels = Labels(info, at)
    gate_o[...] = nn(normed[...], proj[...])
    masked = (labels.valid() * cot[...].astype(F32)).astype(LOW)
    masked_o[...] = masked
    back_o[...] = nt(masked, out_proj[...])
    in_map = maps[:, :state_size]
    out_map = maps[:, state_size:]
    q_at = lax.broadcasted_iota(jnp.int32, (BLOCK, BLOCK), 0)
    s_at = lax.broadcasted_iota(jnp.int32, (BLOCK, BLOCK), 1)
    inside = (q_at >= s_at) & (labels.column() == labels.row())
    scores = jnp.where(inside, nt(out_map, in_map), 0.0)
    lane = lax.broadcasted_iota(jnp.int32, (BLOCK, 2 * head_size), 1)
    run_q = run[...]
    for pair in range(heads // 2):
        span = slice(pair * 2 * head_size, (pair + 1) * 2 * head_size)
        values = scaled[:, span]
        parts = []
        for h in (2 * pair, 2 * pair + 1):
            decay = jnp.exp2(jnp.minimum(run_q[:, h : h + 1] - run_t[0, h : h + 1], 0.0))
            parts.append(nn((scores * decay).astype(LOW), values))
        inner_o[:, span] = jnp.where(lane < head_size, parts[0], parts[1])
    pl.when(at == pl.num_programs(0) - 1)(exchange.finish)


def gate_kernel(
    sizes, info, hid, masked_back, gate, inner, pre, maps, run, state, carry, inbound, out_proj, gain, skip,
    block_o, gated_o, back_o, enter_back_o, gate_back_o, row_o, out_back_o, enter_o, leaving_o, gain_o, skip_o,
    now, leaving, through, skip_row,
):
    inner_width, channels, heads = sizes
    state_size = (channels - inner_width) // 2
    at = pl.program_id(0)
    labels = Labels(info, at)
    groups = head_groups(heads, inner_width)
    pairs = head_groups(heads, inner_width, 2)

    @pl.when(at == 0)
    def _():
        skip_row[...] = spread(jnp.broadcast_to(skip[...], (8, heads)), pairs)
        now[...] = inbound[...].astype(F32)
        leaving[...] = jnp.zeros_like(leaving)
        through[...] = jnp.ones_like(through)
        gain_o[...] = jnp.zeros_like(gain_o)
        skip_o[...] = jnp.zeros_like(skip_o)

    values = silu(pre[...])
    out_map = maps[:, state_size:]
    entry = spread(labels.entry() * jnp.exp2(run[...]), pairs)
    entering = now[...]
    enter_o[0] = entering
    enter_high, enter_rest = halves(entering)
    scanned = inner[...] + entry * nn(out_map, enter_high)
    factor = carry[0, 0:1]
    now[...] = factor * entering + state[0]
    mixer = scanned + skip_row[0:1] * values
    si, si_slope = silu_parts(gate[...])
    gated = mixer * si
    rate = rms_rate(gated)
    unit = gated * rate
    gain_row = gain[...]
    gated_low = (unit * gain_row).astype(LOW)
    gated_o[...] = gated_low
    valid = labels.valid()
    branch = nn(gated_low, out_proj[...])
    block_o[...] = (valid * (hid[...].astype(F32) + branch)).astype(LOW)
    back = masked_back[...]
    product = back * unit
    gain_o[...] += jnp.sum(product, axis=0, keepdims=True)
    mean = jnp.mean(product * gain_row, axis=-1, keepdims=True)
    gated_back = rate * (back * gain_row - unit * mean)
    mixer_back = gated_back * si
    gate_back_o[...] = (gated_back * mixer * si_slope).astype(LOW)
    skip_o[...] += jnp.sum(mixer_back * values, axis=0, keepdims=True)
    back_low = mixer_back.astype(LOW)
    back_o[...] = back_low
    row_o[...] = head_sums(back_low.astype(F32) * scanned, groups)
    back_high, back_rest = halves(entry * mixer_back)
    enter_back_o[...] = back_high
    both = nt(back_high, jnp.concatenate([enter_high, enter_rest], axis=0))
    out_back_o[...] = both[:, :state_size] + both[:, state_size:] + nt(back_rest, enter_high)
    leaving[...] += through[0:1] * tn(out_map, back_high)
    through[...] = through[...] * factor

    @pl.when(at == pl.num_programs(0) - 1)
    def _():
        leaving_o[...] = leaving[...].astype(LOW)


def inner_back_kernel(
    sizes, info, maps, scaled, back, run, run_t, gated, masked, normed, gate_back, leaving, through,
    values_o, maps_o, col_o, out_grad_o, gate_grad_o, onward_o, *scratch
):
    inner_width, channels, heads = sizes
    state_size = (channels - inner_width) // 2
    head_size = inner_width // heads
    at = pl.program_id(0)
    exchange = Exchange(True, lambda: head_groups(heads, inner_width, 2), leaving, through, onward_o, *scratch)
    pl.when(at == 0)(exchange.start)
    pl.when(at == pl.num_programs(0) // 2)(exchange.middle)
    out_grad_o[...] = tn(gated[...], masked[...]).astype(LOW)
    gate_grad_o[...] = tn(normed[...], gate_back[...]).astype(LOW)
    labels = Labels(info, at)
    in_map = maps[:, :state_size]
    out_map = maps[:, state_size:]
    s_at = lax.broadcasted_iota(jnp.int32, (BLOCK, BLOCK), 0)
    q_at = lax.broadcasted_iota(jnp.int32, (BLOCK, BLOCK), 1)
    inside = (q_at >= s_at) & (labels.column() == labels.row())
    scores = jnp.where(inside, nt(in_map, out_map), 0.0)
    lane = lax.broadcasted_iota(jnp.int32, (BLOCK, 2 * head_size), 1)
    run_s = run[...]
    total = jnp.zeros((BLOCK, BLOCK), F32)
    for pair in range(heads // 2):
        span = slice(pair * 2 * head_size, (pair + 1) * 2 * head_size)
        values = scaled[:, span]
        grad = back[:, span]
        parts = []
        for h in (2 * pair, 2 * pair + 1):
            mine = (lane < head_size) == (h % 2 == 0)
            decay = jnp.exp2(jnp.minimum(run_t[0, h : h + 1] - run_s[:, h : h + 1], 0.0))
            parts.append(nn((scores * decay).astype(LOW), grad))
            total += decay * nt(jnp.where(mine, values, jnp.zeros_like(values)), grad)
        values_o[:, span] = jnp.where(lane < head_size, parts[0], parts[1])
    total = jnp.where(inside, total, 0.0).astype(LOW)
    maps_o[:, :state_size] = nn(total, out_map)
    maps_o[:, state_size:] = tn(total, in_map)
    col_o[...] = head_sums(values_o[...] * scaled[...].astype(F32), head_groups(heads, inner_width))
    pl.when(at == pl.num_programs(0) - 1)(exchange.finish)


def finish_kernel(
    sizes, info, pre, maps, scaled, back, enter_back, values_in, maps_in, out_in, col_in, row_in,
    step, run, sig, enter, carry, onward, mixed, mixed_tail, rows, a_log, skip, inner_gain_sum,
    skip_sum, out_grad, gate_grad,
    late_o, late_halo_o, sums_o, out_sum_o, gate_sum_o,
    state, ext, skip_row, local_sem, *scratch
):
    inner_width, channels, heads = sizes
    state_size = (channels - inner_width) // 2
    at = pl.num_programs(0) - 1 - pl.program_id(0)
    first_step = pl.program_id(0) == 0
    last_step = pl.program_id(0) == pl.num_programs(0) - 1

    me = Place()
    grads = [out_grad, gate_grad]
    bufs = [scratch[SCATTER_BUFFERS * a : SCATTER_BUFFERS * (a + 1)] for a in range(2)]

    def part(a, x, core, first, size):
        return grads[a].at[pl.ds((x * CORES + core) * me.seqs + first, size)]

    def source(a):
        return lambda x, first, size: part(a, x, 1 - me.core, first, size)

    scatter = Scatter(me, [source(a) for a in range(2)], bufs, *scratch[2 * SCATTER_BUFFERS :])

    def own(a, x):
        return pltpu.make_async_copy(part(a, x, me.core, 0, me.seqs), bufs[a][1].at[x], local_sem.at[a, x])

    def begin():
        greet(me.around())
        for a in range(2):
            for x in range(me.sx):
                own(a, x).start()
        scatter.send(0, range(me.sz))

    def early():
        for a in range(2):
            for x in range(me.sx):
                own(a, x).wait()
        scatter.absorb(0, range(2))

    points = Points(
        [begin, early, functools.partial(scatter.absorb, 0, range(2, me.sz))]
        + [functools.partial(scatter.absorb, stage, part) for stage in (1, 2) for part in (range(2), range(2, me.sz))],
        2,
    )
    points.hook(0)

    @pl.when(first_step)
    def _():
        state[...] = onward[...].astype(F32)
        ext[0:EDGE] = jnp.zeros((EDGE, channels), F32)
        ext[EDGE + BLOCK :] = jnp.zeros((EDGE, channels), F32)
        sums_o[...] = jnp.zeros_like(sums_o)
        skip_row[...] = spread(jnp.broadcast_to(skip[...], (8, heads)), head_groups(heads, inner_width, 2))

    labels = Labels(info, at)
    group = head_groups(heads, inner_width)
    pairs = head_groups(heads, inner_width, 2)
    taps = rows[0:4]
    act, slope = silu_parts(pre[...])
    values = act[:, :inner_width]
    in_map = maps[:, :state_size]
    out_map = maps[:, state_size:]
    run_q = run[...]
    steps = step[...]
    tail = spread(labels.keep() * jnp.exp2(run_q[BLOCK - 1 :] - run_q), pairs)
    grad = back[...].astype(F32)
    scaled_f = scaled[...].astype(F32)
    state_low = state[...].astype(LOW)
    from_tail = tail * nn(in_map, state_low)
    col_tail = nt((scaled_f * from_tail).astype(LOW), group)
    scaled_back = values_in[...] + from_tail
    step_back = nt((values * scaled_back).astype(LOW), group)
    values_back = spread(steps, pairs) * scaled_back + skip_row[0:1] * grad
    in_back = maps_in[:, :state_size] + nt((tail * scaled_f).astype(LOW), state_low)
    out_back = maps_in[:, state_size:] + out_in[...]
    factor = carry[0, 0:1]
    shared = jnp.sum(enter[0] * state[...], axis=0, keepdims=True) * factor
    shared = row_sums(shared, group)
    state[...] = factor * state[...] + tn(out_map, enter_back[...])
    order = triangle()
    decay_back = (
        tn(order, row_in[...] - col_in[...], HIGHEST) + nn(order, col_tail, HIGHEST) - col_tail + shared
    )
    rate_row = jnp.exp(a_log[...])
    sums_o[7:8, 0:heads] += jnp.sum(decay_back * steps, axis=0, keepdims=True) * -rate_row
    raw_back = (step_back - rate_row * decay_back) * sig[...]
    sums_o[7:8, 128 : 128 + heads] += jnp.sum(raw_back, axis=0, keepdims=True)
    raw_low = raw_back.astype(LOW)
    late_o[:, channels:] = raw_low
    ext[EDGE : EDGE + BLOCK, :inner_width] = values_back * slope[:, :inner_width]
    ext[EDGE : EDGE + BLOCK, inner_width : inner_width + state_size] = (
        in_back * slope[:, inner_width : inner_width + state_size]
    )
    ext[EDGE : EDGE + BLOCK, inner_width + state_size :] = out_back * slope[:, inner_width + state_size :]
    points.hook(1)
    pre_back = ext[EDGE : EDGE + BLOCK]
    inputs = mixed[...]
    sums_o[4:5] += jnp.sum(pre_back, axis=0, keepdims=True)
    sums_o[3:4] += jnp.sum(pre_back * inputs, axis=0, keepdims=True)
    total = taps[3:4] * pre_back
    same = Labels(info, at, BLOCK + EDGE).same()
    for j in (1, 2, 3):
        ahead = same[j : j + BLOCK, j : j + 1] * ext[EDGE + j : EDGE + j + BLOCK]
        sums_o[3 - j : 4 - j] += jnp.sum(ahead * inputs, axis=0, keepdims=True)
        total += taps[3 - j : 4 - j] * ahead
    mixed_low = total.astype(LOW)
    late_o[:, :channels] = mixed_low
    ext[EDGE + BLOCK :] = ext[EDGE : 2 * EDGE]
    @pl.when(last_step)
    def _():
        padded = jnp.concatenate([jnp.zeros((EDGE, 8), F32), same[:EDGE]], axis=0)
        edge = jnp.zeros((EDGE, channels), F32)
        for j in (1, 2, 3):
            ahead = padded[j : j + EDGE, j : j + 1] * ext[j : j + EDGE]
            sums_o[3 - j : 4 - j] += jnp.sum(ahead * mixed_tail[0], axis=0, keepdims=True)
            edge += taps[3 - j : 4 - j] * ahead
        edge_low = jnp.concatenate([jnp.zeros((HALO - EDGE, channels), F32), edge], axis=0).astype(LOW)
        late_halo_o[:, :channels] = edge_low
        late_halo_o[:, channels:] = jnp.zeros((HALO, heads), LOW)
        sums_o[5:6, :inner_width] = inner_gain_sum[...]
        sums_o[7:8, 256 : 256 + heads] = row_sums(skip_sum[...], group)
        for a, out in enumerate((out_sum_o, gate_sum_o)):
            out[...] = scatter.result(a)
        scatter.settle()


def last_kernel(
    sizes, normed, normed_halo, late, late_halo, gate_sum, sums, gain, halo, hid_in, masked_in, gate_back_in, gate_proj_in,
    late_proj_in, proj_o, small_o, hid_o,
    hid, masked, gate_back, gate_proj, late_proj, load_sem, halo_hid, halo_buf, halo_sem, small_buf, small_sem, other,
    *scratch
):
    inner_width, channels, heads = sizes
    me = Place()
    bufs = scratch[:SCATTER_BUFFERS]
    scatter = Scatter(
        me, [lambda x, first, size: other.at[x, pl.ds(first, size)]], [bufs], *scratch[SCATTER_BUFFERS:]
    )
    loads = [
        pltpu.make_async_copy(source, target, load_sem.at[k])
        for k, (source, target) in enumerate(
            (
                (late_proj_in, late_proj), (gate_proj_in, gate_proj), (gate_back_in, gate_back), (hid_in, hid),
                (masked_in, masked),
            )
        )
    ]
    for load in loads:
        load.start()
    greet(me.around() + [me.along(1), me.along(-1)])
    back = remote(halo_hid, halo_buf, halo_sem.at[0], halo_sem.at[1], me.along(-1))

    axes = [
        (CORES, me.core, [(1, 1 - me.core, me.twin)]),
        (me.sx, me.x, [(k, p, me.device(x=p)) for k, p in me.peers("x")]),
        (me.sy, me.y, [(k, p, me.device(y=p)) for k, p in me.peers("y")]),
        (me.sz, me.z, [(k, p, me.device(z=p)) for k, p in me.peers("z")]),
    ]

    def small_copies(stage):
        _, mine, peers = axes[stage]
        buf = small_buf.at[stage, mine]
        return [remote(buf, buf, small_sem.at[0, stage, k], small_sem.at[1, stage, mine], device) for k, _, device in peers]

    def small_send(stage, value):
        small_buf[stage, axes[stage][1]] = value
        for copy in small_copies(stage):
            copy.start()

    def small_take(stage):
        size, _, peers = axes[stage]
        for _, p, _ in peers:
            buf = small_buf.at[stage, p]
            remote(buf, buf, small_sem.at[0, stage, 0], small_sem.at[1, stage, p], me.twin).wait_recv()
        total = small_buf[stage, 0]
        for i in range(1, size):
            total = total + small_buf[stage, i]
        return total

    own_rows = normed.shape[1] // me.count
    half = me.seqs * own_rows
    mine = bufs[1]
    for x in range(me.sx):
        span = slice(2 * half * x, 2 * half * (x + 1))
        grad = tn(normed[:, span], late[...]) + tn(normed_halo[:, span], late_halo[...])
        first = me.core == 0
        here = jnp.where(first, grad[:half], grad[half:])
        there = jnp.where(first, grad[half:], grad[:half])
        for i in range(me.seqs):
            other[x, i] = there[i * own_rows : (i + 1) * own_rows].astype(LOW)
            mine[x, i] = here[i * own_rows : (i + 1) * own_rows].astype(LOW)
        for group in range(me.sz):
            scatter.copies(0, 0, group, x)[0].start()
    gain_row = gain[...]

    def norm_back(normed_back, v):
        rate = rms_rate(v)
        unit = v * rate
        product = normed_back * unit
        mean = jnp.mean(product * gain_row, axis=-1, keepdims=True)
        return rate * (normed_back * gain_row - unit * mean), jnp.sum(product, axis=0, keepdims=True)

    for load in loads:
        load.wait()
    edge, gain_sum = norm_back(nt(late_halo[:, :channels], late_proj[:, :channels]), halo[...].astype(F32))
    halo_hid[...] = edge
    back.start()
    blocks = hid.shape[0] // BLOCK
    pieces = [(stage, [group]) for stage in range(3) for group in range(me.sz)]
    done = 0
    for block in range(blocks):
        here = slice(block * BLOCK, (block + 1) * BLOCK)
        normed_back = nt(gate_back[here], gate_proj[...]) + nt(late[here], late_proj[...])
        rows_back, more = norm_back(normed_back, hid[here].astype(F32))
        gain_sum += more
        result = masked[here].astype(F32) + rows_back
        if block < blocks - 1:
            hid_o[here] = result.astype(LOW)
        until = (block + 1) * 2 * me.sz // blocks
        for stage, group in pieces[done:until]:
            scatter.absorb(stage, group)
        done = until
    small_buf[0, me.core] = sums[...]
    small_buf[0, me.core, 6:7, 0 : normed.shape[1]] = gain_sum
    small_send(0, small_buf[0, me.core])
    for stage in range(3):
        for at, group in pieces[done : done + 1]:
            scatter.absorb(at, group)
        done += 1
        small_send(stage + 1, small_take(stage))
    for stage, group in pieces[done:]:
        scatter.absorb(stage, group)
    back.wait()
    returned = jnp.where(me.seq < me.seqs - 1, halo_buf[...], 0.0)
    hid_o[hid.shape[0] - BLOCK : hid.shape[0] - HALO] = result[: BLOCK - HALO].astype(LOW)
    hid_o[hid.shape[0] - HALO :] = (result[BLOCK - HALO :] + returned).astype(LOW)
    total = small_take(3)
    mine_at = me.row * me.seqs + me.seq

    def own(v, size):
        width = v.shape[1]
        return pltpu.roll(v, lax.rem(width - mine_at * size, width), 1)[:, :size]

    part = channels // me.count
    small_o[0:5, 0:part] = own(total, part)[0:5]
    inner_part = inner_width // me.count
    small_o[5:6, 0:inner_part] = own(total, inner_part)[5:6]
    small_o[6:7, 0:own_rows] = own(total, own_rows)[6:7]
    for k in range(3):
        small_o[7 + k : 8 + k, 0:heads] = total[7:8, 128 * k : 128 * k + heads]
    proj_o[:, :inner_width] = gate_sum[...]
    proj_o[:, inner_width:] = scatter.result(0)
    scatter.settle()
    for stage in range(4):
        for copy in small_copies(stage):
            copy.wait_send()


def tidy_kernel(
    proj, out, small, hid_grad, proj_o, out_o, taps_o, offset_o, inner_gain_o, gain_o, a_log_o, dt_bias_o, skip_o,
    hid_o,
):
    hid_o[...] = hid_grad[...]
    proj_o[...] = proj[...]
    out_o[...] = out[...]
    width, part = taps_o.shape
    taps_o[...] = small[0:width, 0:part]
    for k, ref in enumerate((offset_o, inner_gain_o, gain_o, a_log_o, dt_bias_o, skip_o)):
        ref[...] = small[width + k, 0 : ref.shape[0]]


def struct(shape, dtype=F32):
    return jax.ShapeDtypeStruct(shape, dtype)


def run_kernel(kernel, name, count, ins, outs, scratch=(), flip=False, collective_id=None, aliases=None, before=0):
    def block(i):
        if before:
            return jnp.maximum(i - before, 0)
        return count - 1 - i if flip else i

    def spec(array, kind):
        shape = array.shape
        zeros = (0,) * (len(shape) - 1)
        if kind == "any":
            return pl.BlockSpec(memory_space=pl.ANY)
        if kind == "scalar":
            return pl.BlockSpec(memory_space=pltpu.SMEM)
        if kind == "w":
            return pl.BlockSpec(shape, lambda i: (0,) + zeros)
        if kind == "once":
            return pl.BlockSpec(shape, lambda i: (0,) + zeros, pipeline_mode=pl.Buffered(1))
        if kind == "r":
            return pl.BlockSpec((BLOCK,) + shape[1:], lambda i: (block(i),) + zeros)
        if kind == "b":
            return pl.BlockSpec((1,) + shape[1:], lambda i: (block(i),) + zeros)
        if kind == "c":
            return pl.BlockSpec((shape[0], shape[1] // count), lambda i: (0, i))
        if kind == "part":
            return pl.BlockSpec((shape[0] // count, shape[1]), lambda i: (i, 0))
        if kind[0] == "r":
            return pl.BlockSpec((BLOCK, kind[1]), lambda i: (block(i), 0))
        return pl.BlockSpec(kind, lambda i: (0,) * len(kind))

    return pl.pallas_call(
        kernel,
        name=name,
        grid=(count + before,),
        in_specs=[spec(a, k) for a, k in ins],
        out_specs=[spec(a, k) for a, k in outs],
        out_shape=[a for a, _ in outs],
        scratch_shapes=list(scratch),
        input_output_aliases=aliases or {},
        compiler_params=pltpu.CompilerParams(
            dimension_semantics=("arbitrary",),
            vmem_limit_bytes=VMEM_BYTES,
            collective_id=collective_id,
            has_side_effects=collective_id is not None,
        ),
    )(*[a for a, _ in ins])


def body(
    hidden, lengths, cotangent, norm_gain, in_proj, conv_weight, conv_bias, a_log, dt_bias, skip_weight, inner_gain,
    out_proj,
):
    length, model = hidden.shape[1:]
    count = length // BLOCK
    heads = a_log.shape[0]
    devices = lax.axis_size(AXES)
    seqs = lax.axis_size("seq")
    inner_width = out_proj.shape[0] * devices
    channels = conv_weight.shape[1] * devices
    state_size = (channels - inner_width) // 2
    sizes = (inner_width, channels, heads)
    hid = hidden[0]
    cot = cotangent[0]
    width, part = conv_weight.shape
    own_rows, columns = in_proj.shape
    a_row, bias_row, skip_row = a_log[None], dt_bias[None], skip_weight[None]
    info = jnp.concatenate([lengths, (lax.axis_index("seq") * length).reshape(1, 1)], axis=1)

    late_width = columns - inner_width
    late_width = columns - inner_width
    token = struct((length, inner_width), LOW)
    (
        normed, normed_halo, pre, maps, scaled, mixed, mixed_tail, step, run, run_t, sig, state, carry, final_state,
        through, late_proj, rows, inner_gain_row, gain_row, halo, gate_all, out_all,
    ) = run_kernel(
        functools.partial(project_kernel, sizes), "project", count,
        [
            (info, "scalar"), (hid, "r"), (hid, "any"), (a_row, "w"), (bias_row, "w"), (in_proj, "any"), (out_proj, "any"),
            (conv_weight, "w"), (conv_bias[None], "w"), (inner_gain[None], "w"), (norm_gain[None], "w"),
        ],
        [
            (struct((length, model), LOW), "r"), (struct((HALO, model), LOW), "w"),
            (struct((length, channels)), "r"), (struct((length, 2 * state_size), LOW), "r"),
            (token, "r"), (struct((length, channels)), "r"),
            (struct((count, EDGE, channels)), "b"), (struct((length, heads)), "r"), (struct((length, heads)), "r"),
            (struct((count, heads, BLOCK)), "b"), (struct((length, heads)), "r"),
            (struct((count, state_size, inner_width)), "b"), (struct((count, 8, inner_width)), "b"),
            (struct((state_size, inner_width), LOW), "w"), (struct((8, 128)), "w"),
            (struct((model, late_width), LOW), "w"), (struct((8, channels)), "w"), (struct((1, inner_width)), "w"),
            (struct((1, model)), "w"), (struct((HALO, model), LOW), "w"),
            (struct((devices, own_rows, inner_width), LOW), "any"), (struct((devices,) + out_proj.shape, LOW), "any"),
        ],
        [
            pltpu.VMEM((EDGE + BLOCK, channels), F32), pltpu.VMEM((state_size, inner_width), F32),
            pltpu.VMEM((8, 128), F32), pltpu.VMEM((8, 128), F32), pltpu.VMEM((devices, 8, 128), F32),
            pltpu.VMEM((devices, own_rows, late_width), LOW), pltpu.VMEM((HALO, model), LOW), pltpu.SemaphoreType.DMA((2,)),
        ] + gather_semaphores(2) + gather_semaphores(2),
        collective_id=1,
        before=1,
    )
    out_full = out_all.reshape(inner_width, model)
    gate_proj = gate_all.reshape(model, inner_width)
    pieces = (seqs, state_size // seqs, inner_width)
    gate, inner, masked, masked_back, inbound = run_kernel(
        functools.partial(inner_kernel, sizes), "inner", count,
        [
            (info, "scalar"), (normed, "r"), (gate_proj, "once"), (out_full, "once"), (cot, "r"), (maps, "r"),
            (scaled, "r"), (run, "r"), (run_t, "b"), (final_state.reshape(pieces), "w"), (through, "w"),
        ],
        [
            (struct((length, inner_width)), "r"), (struct((length, inner_width)), "r"), (struct((length, model), LOW), "r"),
            (struct((length, inner_width)), "r"), (struct(pieces, LOW), "w"),
        ],
        exchange_scratch(pieces),
        collective_id=2,
    )
    (
        block_out, gated, back, enter_back, gate_back, row_term, out_in, enter, leaving, inner_gain_sum, skip_sum,
    ) = run_kernel(
        functools.partial(gate_kernel, sizes), "gate", count,
        [
            (info, "scalar"), (hid, "r"), (masked_back, "r"), (gate, "r"), (inner, "r"), (pre, ("r", inner_width)), (maps, "r"),
            (run, "r"), (state, "b"), (carry, "b"), (inbound.reshape(state_size, inner_width), "w"), (out_full, "once"),
            (inner_gain_row, "w"), (skip_row, "w"),
        ],
        [
            (struct((length, model), LOW), "r"), (token, "r"), (token, "r"),
            (token, "r"), (token, "r"), (struct((length, heads)), "r"), (struct((length, state_size)), "r"),
            (struct((count, state_size, inner_width)), "b"), (struct((state_size, inner_width), LOW), "w"),
            (struct((1, inner_width)), "w"), (struct((1, inner_width)), "w"),
        ],
        [
            pltpu.VMEM((state_size, inner_width), F32), pltpu.VMEM((state_size, inner_width), F32),
            pltpu.VMEM((8, inner_width), F32), pltpu.VMEM((8, inner_width), F32),
        ],
    )
    values_in, maps_in, col_in, out_grad, gate_grad, onward = run_kernel(
        functools.partial(inner_back_kernel, sizes), "inner_back", count,
        [
            (info, "scalar"), (maps, "r"), (scaled, "r"), (back, "r"), (run, "r"), (run_t, "b"), (gated, "c"),
            (masked, "w"), (normed, "w"), (gate_back, "c"), (leaving.reshape(pieces), "w"), (through, "w"),
        ],
        [
            (struct((length, inner_width)), "r"), (struct((length, 2 * state_size)), "r"),
            (struct((length, heads)), "r"), (struct((inner_width, model), LOW), "part"),
            (struct((model, inner_width), LOW), "c"), (struct(pieces, LOW), "w"),
        ],
        exchange_scratch(pieces),
        collective_id=3,
    )
    gate_one = (own_rows, inner_width)
    late, late_halo, sums, out_sum, gate_sum = run_kernel(
        functools.partial(finish_kernel, sizes), "finish", count,
        [
            (info, "scalar"), (pre, "r"), (maps, "r"), (scaled, "r"),
            (back, "r"), (enter_back, "r"), (values_in, "r"), (maps_in, "r"), (out_in, "r"), (col_in, "r"),
            (row_term, "r"), (step, "r"), (run, "r"), (sig, "r"), (enter, "b"), (carry, "b"),
            (onward.reshape(state_size, inner_width), "w"), (mixed, "r"), (mixed_tail, "b"),
            (rows, "w"), (a_row, "w"), (skip_row, "w"), (inner_gain_sum, "w"), (skip_sum, "w"),
            (out_grad.reshape(devices, -1, model), "any"), (gate_grad.reshape(devices, -1, inner_width), "any"),
        ],
        [
            (struct((length, late_width), LOW), "r"), (struct((HALO, late_width), LOW), "w"),
            (struct((8, channels)), "w"), (struct(out_proj.shape), "w"), (struct(gate_one), "w"),
        ],
        [
            pltpu.VMEM((state_size, inner_width), F32), pltpu.VMEM((2 * EDGE + BLOCK, channels), F32),
            pltpu.VMEM((8, inner_width), F32), pltpu.SemaphoreType.DMA((2, lax.axis_size("row") // CORES)),
        ] + scatter_scratch([out_proj.shape, gate_one]),
        flip=True,
        collective_id=4,
    )
    late_one = (own_rows, late_width)
    most = max(CORES, lax.axis_size("row") // CORES, DEPTH, seqs // DEPTH)
    sx = lax.axis_size("row") // CORES
    proj_sum, small_sums, hid_grad = run_kernel(
        functools.partial(last_kernel, sizes), "last", 1,
        [
            (normed, "once"), (normed_halo, "w"), (late, "once"), (late_halo, "w"), (gate_sum, "w"), (sums, "w"),
            (gain_row, "w"), (halo, "w"), (hid, "any"), (masked, "any"), (gate_back, "any"), (gate_proj, "any"),
            (late_proj, "any"),
        ],
        [(struct(in_proj.shape), "w"), (struct((16, 128)), "w"), (struct((length, model), LOW), "w")],
        [
            pltpu.VMEM(hid.shape, LOW), pltpu.VMEM(hid.shape, LOW), pltpu.VMEM(gate_back.shape, LOW),
            pltpu.VMEM(gate_proj.shape, LOW), pltpu.VMEM(late_proj.shape, LOW), pltpu.SemaphoreType.DMA((5,)),
            pltpu.VMEM((HALO, model), F32), pltpu.VMEM((HALO, model), F32), pltpu.SemaphoreType.DMA((2,)),
            pltpu.VMEM((4, most, 8, channels), F32),
            pltpu.SemaphoreType.DMA((2, 4, most)), pltpu.VMEM((sx, seqs) + late_one, LOW),
        ] + scatter_scratch([late_one]),
        collective_id=5,
    )
    proj_grad, out_proj_grad, taps_grad, offset_grad, inner_grad, gain_grad, a_log_grad, dt_grad, skip_grad, hid_grad = (
        run_kernel(
            tidy_kernel, "tidy", 1,
            [(proj_sum, "w"), (out_sum, "w"), (small_sums, "w"), (hid_grad, "w")],
            [
                (struct(in_proj.shape), "w"), (struct(out_proj.shape), "w"), (struct((width, part)), "w"),
                (struct((part,)), "w"), (struct(inner_gain.shape), "w"), (struct(norm_gain.shape), "w"),
                (struct((heads,)), "w"), (struct((heads,)), "w"), (struct((heads,)), "w"),
                (struct((length, model), LOW), "w"),
            ],
        )
    )
    return (
        block_out[None], hid_grad[None], gain_grad, proj_grad, taps_grad, offset_grad, a_log_grad, dt_grad, skip_grad,
        inner_grad, out_proj_grad,
    )


def solution(mesh):
    weights = P(AXES)
    tokens = P("row", "seq", None)
    rows = P(AXES, None)
    return jax.shard_map(
        body,
        mesh=mesh,
        in_specs=(
            tokens, P("row", None), tokens, weights, rows, P(None, AXES), weights, P(), P(), P(), weights, rows,
        ),
        out_specs=(tokens, tokens, weights, rows, P(None, AXES), weights, P(), P(), P(), weights, rows),
        check_vma=False,
    )
```

```python
import functools

import jax
import jax.numpy as jnp
from jax import lax
from jax.experimental import pallas as pl
from jax.experimental.pallas import tpu as pltpu
from jax.sharding import PartitionSpec as P

BLOCK = 256
EPS = 1e-05
LOG2E = 1.4426950408889634
HIGHEST = lax.Precision.HIGHEST
F32 = jnp.float32
LOW = jnp.bfloat16
EDGE = 8
HALO = 16
BAND = 64
AXES = ("row", "seq")
MESH = pl.DeviceIdType.MESH
CORES = 2
DEPTH = 4
VMEM_BYTES = 63 * 1024 * 1024


def nn(a, b, precision=None):
    return lax.dot_general(
        a, b, (((1,), (0,)), ((), ())), precision=precision, preferred_element_type=F32
    )


def nt(a, b):
    return lax.dot_general(a, b, (((1,), (1,)), ((), ())), preferred_element_type=F32)


def tn(a, b, precision=None):
    return lax.dot_general(
        a, b, (((0,), (0,)), ((), ())), precision=precision, preferred_element_type=F32
    )


def halves(v):
    high = v.astype(LOW)
    return high, (v - high.astype(F32)).astype(LOW)


def head_groups(heads, width, copies=1):
    column = lax.broadcasted_iota(jnp.int32, (copies * heads, width), 1)
    first = lax.rem(lax.broadcasted_iota(jnp.int32, (copies * heads, width), 0), heads) * (width // heads)
    return ((column >= first) & (column < first + width // heads)).astype(F32).astype(LOW)


def spread(v, pairs):
    return nn(jnp.concatenate(halves(v), axis=1), pairs)


def head_sums(v, groups):
    high, rest = halves(v)
    return nt(high, groups) + nt(rest, groups)


def row_sums(v, groups):
    wide = jnp.concatenate([jnp.broadcast_to(part, (16, v.shape[1])) for part in halves(v)], axis=0)
    sums = nt(wide, groups)
    return sums[0:1] + sums[16:17]


def triangle():
    return (
        lax.broadcasted_iota(jnp.int32, (BLOCK, BLOCK), 0) >= lax.broadcasted_iota(jnp.int32, (BLOCK, BLOCK), 1)
    ).astype(F32)


def sigmoid(v):
    return 0.5 + 0.5 * jnp.tanh(0.5 * v)


def silu(v):
    half = 0.5 * v
    return half + half * jnp.tanh(half)


def silu_parts(v):
    half = 0.5 * v
    curve = jnp.tanh(half)
    value = half + half * curve
    rate = 0.5 + 0.5 * curve
    return value, rate + value - value * rate


def log1p_of(v):
    series = v * (1.0 - v * (0.5 - v * (1.0 / 3.0 - 0.25 * v)))
    return jnp.where(v < 0.01, series, jnp.log(1.0 + v))


def rms_rate(v):
    return lax.rsqrt(jnp.mean(v * v, axis=-1, keepdims=True) + EPS)


def bands():
    return [slice(at, at + BAND) for at in range(0, BLOCK, BAND)]


def shifted(rows, by):
    return slice(rows.start + by, rows.stop + by)


def columns_of(width):
    return [slice(at, at + 128) for at in range(0, width, 128)]


def fold_rows(v):
    return sum(v[at : at + 8] for at in range(0, v.shape[0], 8))


def wide_columns(table, count, buf):
    for j in range(count):
        buf[j] = jnp.broadcast_to(table[:, j : j + 1], (table.shape[0], 128))


class Labels:
    def __init__(self, info, block, rows=BLOCK):
        slots = info.shape[1] - 1
        self.ends, total = [], 0
        for i in range(slots):
            total = total + info[0, i]
            self.ends.append(total)
        self.base = info[0, slots] + block * BLOCK
        self.rows = rows

    def of(self, place):
        total = sum((place >= end).astype(jnp.int32) for end in self.ends)
        return jnp.where(place < 0, -1, total)

    def column(self):
        return self.of(self.base + lax.broadcasted_iota(jnp.int32, (self.rows, 1), 0))

    def row(self):
        return self.of(self.base + lax.broadcasted_iota(jnp.int32, (1, self.rows), 1))

    def before(self):
        return self.of(self.base - 1)

    def last(self):
        return self.of(self.base + BLOCK - 1)

    def entry(self):
        return (self.column() == self.before()).astype(F32)

    def keep(self):
        return (self.column() == self.last()).astype(F32)

    def flag(self):
        return (jnp.full((8, 128), self.before(), jnp.int32) == self.last()).astype(F32)

    def valid(self):
        place = self.base + lax.broadcasted_iota(jnp.int32, (self.rows, 1), 0)
        return (place < self.ends[-1]).astype(F32)

    def same(self):
        shape = (self.rows, 8)
        place = self.base + lax.broadcasted_iota(jnp.int32, shape, 0)
        own = self.of(place)
        return (self.of(place - lax.broadcasted_iota(jnp.int32, shape, 1)) == own).astype(F32)


class Place:
    def __init__(self):
        rows, self.seqs = lax.axis_size("row"), lax.axis_size("seq")
        self.sx, self.sz = rows // CORES, DEPTH
        self.sy = self.seqs // DEPTH
        row, seq = lax.axis_index("row"), lax.axis_index("seq")
        self.x, self.core = lax.div(row, CORES), lax.rem(row, CORES)
        self.z, self.y = lax.div(seq, self.sy), lax.rem(seq, self.sy)
        self.row, self.seq = row, seq
        self.count = rows * self.seqs
        self.twin = self.device(core=1 - self.core)

    def device(self, x=None, core=None, z=None, y=None):
        x = self.x if x is None else x
        core = self.core if core is None else core
        z = self.z if z is None else z
        y = self.y if y is None else y
        return {"row": x * CORES + core, "seq": z * self.sy + y}

    def slot(self, x=None, core=None, z=None, y=None):
        at = self.device(x, core, z, y)
        return at["row"] * self.seqs + at["seq"]

    def peers(self, axis):
        size, mine = {"x": (self.sx, self.x), "y": (self.sy, self.y), "z": (self.sz, self.z)}[axis]
        return [(k, lax.rem(mine + k, size)) for k in range(1, size)]

    def around(self):
        return (
            [self.device(x=p) for _, p in self.peers("x")]
            + [self.device(y=p) for _, p in self.peers("y")]
            + [self.device(z=p) for _, p in self.peers("z")]
            + [self.twin]
        )

    def along(self, by):
        return {"seq": lax.rem(self.seq + by + self.seqs, self.seqs)}


def greet(devices):
    barrier = pltpu.get_barrier_semaphore()
    for device in devices:
        pl.semaphore_signal(barrier, inc=1, device_id=device, device_id_type=MESH)
    pl.semaphore_wait(barrier, len(devices))


def remote(source, target, send_sem, recv_sem, device):
    return pltpu.make_async_remote_copy(
        src_ref=source, dst_ref=target, send_sem=send_sem, recv_sem=recv_sem, device_id=device, device_id_type=MESH
    )


def guarded(act, when):
    if when is None:
        act()
    else:
        pl.when(when)(act)


class Gather:
    def __init__(self, me, ins, outs, local_sem, send_sem, recv_sem):
        self.me, self.ins, self.outs = me, ins, outs
        self.local_sem, self.send_sem, self.recv_sem = local_sem, send_sem, recv_sem
        self.steps = [self.plan(point) for point in range(7)]

    def plan(self, point):
        me = self.me
        xs = [p for _, p in me.peers("x")]
        ys = [p for _, p in me.peers("y")]
        above, below = me.z + 1 < me.sz, me.z > 0
        up, down = (me.device(z=me.z + 1), above), (me.device(z=me.z - 1), below)
        around = [(me.device(y=p), None) for p in ys] + [(me.device(x=p), None) for p in xs] + [(me.twin, None)]
        if point == 0:
            return [(None, None, [up, down] + around)]
        if point < me.sz:
            found = []
            for z, comes, on in ((me.z - point, me.z >= point, up), (me.z + point, me.z + point < me.sz, down)):
                on = (on[0], jnp.logical_and(comes, on[1]))
                found.append((me.slot(z=z), comes, [on] + [(device, comes) for device, _ in around]))
            return found
        found = []
        turns = [lax.rem(me.z + k, me.sz) for k in range(me.sz)]
        first, last = {4: (0, 2), 5: (2, 4), 6: (0, 4)}[point]
        for z in turns[first:last]:
            even = lax.rem(z, 2) == 0
            if point < 6:
                for y in ys:
                    found.append((me.slot(z=z, y=y), None, [(me.device(x=p), even) for p in xs] + [(me.twin, None)]))
                for x in xs:
                    to = [(me.device(y=p), jnp.logical_not(even)) for p in ys] + [(me.twin, None)]
                    found.append((me.slot(z=z, x=x), None, to))
            else:
                for y in ys:
                    for x in xs:
                        found.append((me.slot(z=z, x=x, y=y), None, [(me.twin, None)]))
        return found

    def copies(self, a, point):
        index = sum(len(to) for earlier in self.steps[:point] for _, _, to in earlier)
        found = []
        for slot, comes, to in self.steps[point]:
            at = self.me.slot() if slot is None else slot
            source = self.ins[a] if slot is None else self.outs[a].at[at]
            group = []
            for device, when in to:
                group.append(
                    (remote(source, self.outs[a].at[at], self.send_sem.at[a, index], self.recv_sem.at[a, at], device), when)
                )
                index += 1
            found.append((slot, comes, group))
        return found

    def arrived(self, a, slot, comes=None):
        block = self.outs[a].at[slot]
        guarded(remote(block, block, self.send_sem.at[a, 0], self.recv_sem.at[a, slot], self.me.twin).wait_recv, comes)

    def own(self, a):
        return pltpu.make_async_copy(self.ins[a], self.outs[a].at[self.me.slot()], self.local_sem.at[a])

    def run(self, point):
        for a in range(len(self.ins)):
            if point == 0:
                self.own(a).start()
            for slot, comes, group in self.copies(a, point):
                if slot is not None:
                    self.arrived(a, slot, comes)
                for copy, when in group:
                    guarded(copy.start, when)

    def finish(self, a):
        me = self.me
        for x in range(me.sx):
            for seq in range(me.seqs):
                self.arrived(a, (x * CORES + 1 - me.core) * me.seqs + seq)
        self.own(a).wait()

    def settle(self):
        for a in range(len(self.ins)):
            for point in range(7):
                for _, _, group in self.copies(a, point):
                    for copy, when in group:
                        guarded(copy.wait_send, when)


def gather_semaphores(arrays):
    devices = lax.axis_size(AXES)
    return [
        pltpu.SemaphoreType.DMA((arrays,)),
        pltpu.SemaphoreType.DMA((arrays, 4 * devices)),
        pltpu.SemaphoreType.DMA((arrays, devices)),
    ]


class Exchange:
    def __init__(self, reverse, group, state, through, out, parts, factors, ready, sems):
        self.reverse, self.group = reverse, group
        self.state, self.through, self.out = state, through, out
        self.parts, self.factors, self.ready, self.sems = parts, factors, ready, sems
        self.size, self.mine = lax.axis_size("seq"), lax.axis_index("seq")

    def copy(self, source, target, kind, index_out, index_in, peer):
        return remote(source, target, self.sems.at[kind, index_out], self.sems.at[kind + 1, index_in], {"seq": peer})

    def first(self):
        found = []
        for k in range(1, self.size):
            peer = lax.rem(self.mine + k, self.size)
            found.append(self.copy(self.through, self.factors.at[self.mine], 2, k, self.mine, peer))
            found.append(self.copy(self.state.at[peer], self.parts.at[self.mine], 0, k, self.mine, peer))
        return found

    def result(self, j):
        return self.copy(self.ready.at[j], self.out.at[self.mine], 4, j, self.mine, j)

    def start(self):
        for copy in self.first():
            copy.start()
        self.parts[self.mine] = self.state[self.mine]
        self.factors[self.mine] = self.through[...]

    def others(self):
        return [{"seq": lax.rem(self.mine + k, self.size)} for k in range(1, self.size)]

    def middle(self):
        group = self.group()
        heads = group.shape[0] // 2
        total = jnp.zeros(self.state.shape[1:], F32)
        for k in range(self.size):
            j = self.size - 1 - k if self.reverse else k
            self.ready[j] = total.astype(LOW)

            @pl.when(self.mine != j)
            def _(j=j):
                self.result(j).start()
                self.copy(self.through, self.factors.at[j], 2, 0, j, j).wait_recv()
                self.copy(self.state.at[0], self.parts.at[j], 0, 0, j, j).wait_recv()

            factor = spread(self.factors[j][:, :heads], group)
            total = factor[0:1] * total + self.parts[j].astype(F32)
        self.out[self.mine] = self.ready[self.mine]

    def landed(self):
        pieces = self.out[...].astype(F32)
        return pieces.reshape(pieces.shape[0] * pieces.shape[1], pieces.shape[2])

    def finish(self):
        for k in range(1, self.size):
            j = lax.rem(self.mine + k, self.size)
            self.copy(self.ready.at[j], self.out.at[j], 4, j, j, j).wait_recv()
        for copy in self.first():
            copy.wait_send()
        for j in range(self.size):
            pl.when(self.mine != j)(self.result(j).wait_send)


EXCHANGE_BUFFERS = 5


def exchange_scratch(pieces):
    size = pieces[0]
    return [
        pltpu.VMEM(pieces, LOW), pltpu.VMEM(pieces, LOW), pltpu.VMEM((size, 8, 128), F32), pltpu.VMEM(pieces, LOW),
        pltpu.SemaphoreType.DMA((6, size)),
    ]


def add_slots(target, first, source, start, pieces):
    def step(i, _):
        at = first + i
        target[at] = (target[at].astype(F32) + source[start + i].astype(F32)).astype(target.dtype)
        return 0

    lax.fori_loop(0, pieces, step, 0)


class Scatter:
    def __init__(self, me, grads, bufs, send_sem, recv_sem):
        self.me, self.grads, self.bufs = me, grads, bufs
        self.send_sem, self.recv_sem = send_sem, recv_sem
        self.groups = [(k, lax.rem(me.z + k, me.sz)) for k in list(range(1, me.sz)) + [0]]

    def own(self, a, x):
        return self.grads[a].at[x * CORES + self.me.core]

    def plan(self, a, stage, group):
        me = self.me
        sx, sy = me.sx, me.sy
        twin_buf, from_x, from_y, from_y2, from_x2, from_z = self.bufs[a]
        xs, ys = me.peers("x"), me.peers("y")
        k, z = self.groups[group]
        along_x = k % 2 == 0
        if stage == 0:
            return [
                (
                    self.grads[a].at[x * CORES + 1 - me.core, pl.ds(z * sy, sy)], twin_buf.at[x, pl.ds(z * sy, sy)], x,
                    me.twin,
                )
                for x in range(sx)
            ]
        if stage == 1 and along_x:
            return [
                (self.own(a, x).at[pl.ds(z * sy, sy)], from_x.at[i - 1, k], sx + i - 1, me.device(x=x)) for i, x in xs
            ]
        if stage == 1:
            return [
                (self.own(a, x).at[z * sy + y], from_y.at[i - 1, k, x], sx + (i - 1) * sx + x, me.device(y=y))
                for i, y in ys
                for x in range(sx)
            ]
        start = sx + max(sx - 1, (sy - 1) * sx)
        if stage == 2 and along_x:
            return [
                (self.own(a, me.x).at[z * sy + y], from_y2.at[i - 1, k], start + i - 1, me.device(y=y)) for i, y in ys
            ]
        if stage == 2:
            return [
                (self.own(a, x).at[z * sy + me.y], from_x2.at[i - 1, k], start + i - 1, me.device(x=x)) for i, x in xs
            ]
        if k == 0:
            return []
        start += max(sx - 1, sy - 1)
        return [(self.own(a, me.x).at[z * sy + me.y], from_z.at[k - 1], start, me.device(z=z))]

    def copies(self, a, stage, group, only=None):
        k = self.groups[group][0]
        return [
            remote(source, target, self.send_sem.at[a, k, number], self.recv_sem.at[a, k, number], device)
            for source, target, number, device in self.plan(a, stage, group)
            if only is None or number == only
        ]

    def begin(self, a):
        for group in range(len(self.groups)):
            for copy in self.copies(a, 0, group):
                copy.start()

    def absorb(self, a, stage, group):
        me = self.me
        sy = me.sy
        twin_buf, from_x, from_y, from_y2, from_x2, from_z = self.bufs[a]
        k, z = self.groups[group]
        for copy in self.copies(a, stage, group):
            copy.wait_recv()
        if stage == 0:
            for x in range(me.sx):
                add_slots(self.own(a, x), z * sy, twin_buf.at[x], z * sy, sy)
        elif stage == 1 and k % 2 == 0:
            for i in range(me.sx - 1):
                add_slots(self.own(a, me.x), z * sy, from_x.at[i, k], 0, sy)
        elif stage == 1:
            for i in range(sy - 1):
                for x in range(me.sx):
                    add_slots(self.own(a, x), z * sy + me.y, from_y.at[i, k], x, 1)
        else:
            source = from_y2 if k % 2 == 0 else from_x2
            for i in range((sy if k % 2 == 0 else me.sx) - 1):
                add_slots(self.own(a, me.x), z * sy + me.y, source.at[i], k, 1)
        for copy in self.copies(a, stage + 1, group):
            copy.start()

    def stages(self, a):
        def stage(number):
            for group in range(len(self.groups)):
                self.absorb(a, number, group)

        return [functools.partial(self.begin, a)] + [functools.partial(stage, number) for number in range(3)]

    def result(self, a):
        me = self.me
        from_z = self.bufs[a][5]
        result = self.own(a, me.x)[me.z * me.sy + me.y].astype(F32)
        for group, (k, _) in enumerate(self.groups):
            if k:
                for copy in self.copies(a, 3, group):
                    copy.wait_recv()
                result = result + from_z[k - 1].astype(F32)
        return result

    def settle(self):
        for a in range(len(self.grads)):
            for stage in range(4):
                for group in range(len(self.groups)):
                    for copy in self.copies(a, stage, group):
                        copy.wait_send()


SCATTER_BUFFERS = 6


def scatter_scratch(ones, dtype=LOW):
    rows, seqs = lax.axis_size("row"), lax.axis_size("seq")
    sx, sz, sy = rows // CORES, DEPTH, seqs // DEPTH
    scratch = []
    for one in ones:
        for lead in ((sx, seqs), (sx - 1, sz, sy), (sy - 1, sz, sx), (sy - 1, sz), (sx - 1, sz), (sz - 1,)):
            scratch.append(pltpu.VMEM(lead + tuple(one), dtype))
    most = sx + max(sx - 1, (sy - 1) * sx) + max(sx - 1, sy - 1) + 1
    return scratch + [pltpu.SemaphoreType.DMA((len(ones), sz, most))] * 2


class Stream:
    def __init__(self, source, buf, sem):
        self.source, self.buf, self.sem = source, buf, sem

    def copy(self, block, slot):
        if len(self.source.shape) == 2:
            part = self.source.at[pl.ds(pl.multiple_of(block * BLOCK, BLOCK), BLOCK)]
        else:
            part = self.source.at[pl.ds(block, 1)]
        return pltpu.make_async_copy(part, self.buf.at[slot], self.sem.at[slot])

    def start(self, block, slot):
        self.copy(block, slot).start()

    def wait(self, slot):
        self.copy(0, slot).wait()


def stream_scratch(array):
    one = (BLOCK,) + array.shape[1:] if array.ndim == 2 else (1,) + array.shape[1:]
    return [pltpu.VMEM((2,) + one, array.dtype), pltpu.SemaphoreType.DMA((2,))]


class Points:
    def __init__(self, acts, places, hooks):
        self.acts, self.places, self.hooks = acts, places, hooks

    def hook(self, number):
        for act, place in zip(self.acts, self.places):
            if place % self.hooks == number:
                pl.when(pl.program_id(0) == place // self.hooks)(act)


def project_kernel(
    sizes, count, info, hid, hid_all, a_log, dt_bias, in_proj, out_proj, taps, offset, inner_gain, gain,
    normed_o, normed_halo_o, pre_o, values_o, maps_o, scaled_o, mixed_o, tail_o, step_o, run_o, run_t_o, sig_o,
    state_o, carry_o, final_o, through_o, late_o, rows_o, inner_gain_o, gain_o, halo_o, gate_all, out_all,
    ext, state, through, steps_wide, tails_wide, weighted_buf, same_buf, small, small_all, late_all, halo_buf, halo_sem, *sems
):
    inner_width, channels, heads = sizes
    state_size = (channels - inner_width) // 2
    at = pl.program_id(0) - 1
    me = Place()
    width, part = taps.shape
    own_rows = in_proj.shape[0]
    late_part = in_proj.at[:, pl.ds(inner_width, in_proj.shape[1] - inner_width)]
    gate_part = in_proj.at[:, pl.ds(0, inner_width)]
    now = Gather(me, [small, late_part], [small_all, late_all], *sems[:3])
    later = Gather(me, [gate_part, out_proj], [gate_all, out_all], *sems[3:])

    @pl.when(at < 0)
    def _():
        small[...] = jnp.zeros_like(small)
        small[0:width, 0:part] = taps[...].astype(F32)
        for k, piece in enumerate((offset, inner_gain, gain)):
            small[width + k : width + k + 1, 0 : piece.shape[1]] = piece[...].astype(F32)
        greet(me.around() + [me.along(1), me.along(-1)])
        last = hid_all.at[pl.ds(hid_all.shape[0] - HALO, HALO)]
        halo = remote(last, halo_buf, halo_sem.at[0], halo_sem.at[1], me.along(1))
        halo.start()
        for point in range(4):
            now.run(point)
        later.run(0)
        for point in range(4, 7):
            now.run(point)
        later.run(1)
        now.finish(0)
        for d in range(small_all.shape[0]):
            rows_o[0 : width + 1, d * part : (d + 1) * part] = small_all[d, 0 : width + 1, 0:part]
            for k, (out, piece) in enumerate(((inner_gain_o, inner_gain), (gain_o, gain))):
                size = piece.shape[1]
                out[:, d * size : (d + 1) * size] = small_all[d, width + 1 + k : width + 2 + k, 0:size]
        halo.wait()
        halo_o[...] = jnp.where(me.seq > 0, halo_buf[...].astype(F32), 0.0).astype(LOW)
        now.finish(1)
        for d in range(small_all.shape[0]):
            late_o[d * own_rows : (d + 1) * own_rows] = late_all[d]

    @pl.when(at >= 0)
    def _():
        project_step(
            sizes, info, hid, halo_o, late_o, gain_o, rows_o, a_log, dt_bias,
            normed_o, normed_halo_o, pre_o, values_o, maps_o, scaled_o, mixed_o, tail_o, step_o, run_o, run_t_o, sig_o,
            state_o, carry_o, final_o, through_o, ext, state, through, steps_wide, tails_wide, weighted_buf, same_buf, at,
            Points(
                [functools.partial(later.run, point) for point in range(2, 7)],
                [2 + point * 2 * count // 5 for point in range(5)], 2,
            ),
        )

    @pl.when(at == pl.num_programs(0) - 2)
    def _():
        for a in range(2):
            later.finish(a)
        now.settle()
        later.settle()


def project_step(
    sizes, info, hid, halo, late, gain, rows, a_log, dt_bias,
    normed_o, normed_halo_o, pre_o, values_o, maps_o, scaled_o, mixed_o, tail_o, step_o, run_o, run_t_o, sig_o,
    state_o, carry_o, final_o, through_o, ext, state, through, steps_wide, tails_wide, weighted_buf, same_buf, at, points,
):
    inner_width, channels, heads = sizes
    state_size = (channels - inner_width) // 2
    points.hook(0)
    gain_row = gain[...]

    def norm(v):
        v = v.astype(F32)
        return (v * rms_rate(v) * gain_row).astype(LOW)

    weight = late[:, :channels]

    @pl.when(at == 0)
    def _():
        before = norm(halo[...])
        normed_halo_o[...] = before
        ext[0:EDGE] = nn(before, weight)[HALO - EDGE :]
        state[...] = jnp.zeros_like(state)
        through[...] = jnp.ones_like(through)

    labels = Labels(info, at)
    pairs = head_groups(heads, inner_width, 2)
    normed = norm(hid[...])
    normed_o[...] = normed
    mixed = nn(normed, weight)
    raw = nn(normed, late[:, channels:])
    ext[EDGE:] = mixed
    tail_o[0] = ext[0:EDGE]
    mixed_o[...] = mixed
    wide_columns(labels.same(), 4, same_buf)
    z = raw + dt_bias[...]
    step = jnp.maximum(z, 0.0) + log1p_of(jnp.exp(-jnp.abs(z)))
    log_decay = step * (-LOG2E * jnp.exp(a_log[...]))
    run = nn(triangle(), log_decay, HIGHEST)
    step_o[...] = step
    run_o[...] = run
    sig_o[...] = sigmoid(z)
    wide = jnp.concatenate([run, jnp.zeros((BLOCK, 128 - heads), F32)], axis=1)
    run_t_o[0] = jnp.transpose(wide)[:heads]
    last = run[BLOCK - 1 :]
    tail = labels.keep() * jnp.exp2(last - run)
    steps_wide[...] = spread(step, pairs)
    tails_wide[...] = spread(tail, pairs)
    points.hook(1)
    for cols in columns_of(channels):
        for here in bands():
            total = rows[4:5, cols] + rows[3:4, cols] * ext[shifted(here, EDGE), cols]
            for j in (1, 2, 3):
                total += rows[3 - j : 4 - j, cols] * (same_buf[j, here] * ext[shifted(here, EDGE - j), cols])
            pre_o[here, cols] = total
            act = silu(total)
            if cols.start < inner_width:
                values_o[here, cols] = act
                scaled = steps_wide[here, cols] * act
                scaled_o[here, cols] = scaled.astype(LOW)
                weighted_buf[here, cols] = (tails_wide[here, cols] * scaled).astype(LOW)
            else:
                maps_o[here, cols.start - inner_width : cols.stop - inner_width] = act.astype(LOW)
    ext[0:EDGE] = ext[BLOCK:]
    maps = maps_o[...]
    weighted = weighted_buf[...]
    fresh = tn(maps[:, :state_size], weighted)
    state_o[0] = fresh
    factor = labels.flag()[:, :heads] * jnp.exp2(jnp.broadcast_to(last, (8, heads)))
    through[:, :heads] = through[:, :heads] * factor
    factor = spread(factor, pairs)
    carry_o[0] = factor
    state[...] = factor[0:1] * state[...] + fresh

    @pl.when(at == pl.num_programs(0) - 2)
    def _():
        final_o[...] = state[...].astype(LOW)
        through_o[...] = through[...]


def mix_kernel(
    sizes, count, info, normed, proj_in, out_proj_in, gain, cot, maps, scaled, run, run_t, final, through_in,
    hid_in, values_in, state_in, carry, skip,
    masked_o, block_o, gated_o, back_o, enter_back_o, gate_back_o, row_o, out_back_o, enter_o, leaving_o, gain_o, skip_o,
    proj, out_proj, load_sem, hid_buf, hid_sem, values_buf, values_sem, state_buf, state_sem,
    inner_all, gate_all, back_all,
    now, leaving, through, skip_row, entry, scan, unit_buf, slope_buf, gain_buf, skip_sum, prod_high, prod_rest, back_rest,
    *scratch
):
    inner_width, channels, heads = sizes
    step = pl.program_id(0)
    exchange = Exchange(False, lambda: head_groups(heads, inner_width, 2), final, through_in, *scratch)
    loads = [
        pltpu.make_async_copy(proj_in, proj, load_sem.at[0]), pltpu.make_async_copy(out_proj_in, out_proj, load_sem.at[1])
    ]
    streams = [
        Stream(hid_in, hid_buf, hid_sem), Stream(values_in, values_buf, values_sem), Stream(state_in, state_buf, state_sem)
    ]

    @pl.when(step == 0)
    def _():
        for load in loads:
            load.start()
        greet(exchange.others())
        exchange.start()

    pl.when(step == count // 2)(exchange.middle)

    @pl.when(step < count)
    def _():
        inner_step(
            sizes, info, normed, proj, out_proj, gain, cot, maps, scaled, run, run_t, masked_o,
            inner_all.at[step], gate_all.at[step], back_all.at[step], step, loads,
        )

    @pl.when(step == count - 1)
    def _():
        for stream in streams:
            stream.start(0, 0)

    @pl.when(step == count)
    def _():
        exchange.finish()
        now[...] = exchange.landed()
        skip_row[...] = spread(jnp.broadcast_to(skip[...], (8, heads)), head_groups(heads, inner_width, 2))
        leaving[...] = jnp.zeros_like(leaving)
        through[...] = jnp.ones_like(through)
        gain_buf[...] = jnp.zeros_like(gain_buf)
        skip_sum[...] = jnp.zeros_like(skip_sum)

    @pl.when(step >= count)
    def _():
        at = step - count
        slot = lax.rem(at, 2)
        for stream in streams:
            stream.wait(slot)

        @pl.when(at < count - 1)
        def _():
            for stream in streams:
                stream.start(at + 1, 1 - slot)

        hid, values, state = (stream.buf.at[slot] for stream in streams)
        gate_step(
            sizes, info, hid, back_all.at[at], gate_all.at[at], inner_all.at[at], values, maps, run, state, carry, out_proj,
            gain, block_o, gated_o, back_o, enter_back_o, gate_back_o, row_o, out_back_o, enter_o,
            now, leaving, through, skip_row, entry, scan, unit_buf, slope_buf, gain_buf, skip_sum, prod_high, prod_rest,
            back_rest, at,
        )

    @pl.when(step == 2 * count - 1)
    def _():
        leaving_o[...] = leaving[...].astype(LOW)
        gain_o[...] = jnp.sum(gain_buf[...], axis=0, keepdims=True) / gain[...]
        skip_o[...] = jnp.sum(skip_sum[...], axis=0, keepdims=True)


def inner_step(
    sizes, info, normed, proj, out_proj, gain, cot, maps, scaled, run, run_t, masked_o, inner_o, gate_o, back_o, at, loads
):
    inner_width, channels, heads = sizes
    state_size = (channels - inner_width) // 2
    head_size = inner_width // heads
    labels = Labels(info, at)
    in_map = maps[:, :state_size]
    out_map = maps[:, state_size:]
    q_at = lax.broadcasted_iota(jnp.int32, (BLOCK, BLOCK), 0)
    s_at = lax.broadcasted_iota(jnp.int32, (BLOCK, BLOCK), 1)
    inside = (q_at >= s_at) & (labels.column() == labels.row())
    scores = jnp.where(inside, nt(out_map, in_map), 0.0)
    lane = lax.broadcasted_iota(jnp.int32, (BLOCK, 2 * head_size), 1)
    run_q = run[...]
    for pair in range(heads // 2):
        span = slice(pair * 2 * head_size, (pair + 1) * 2 * head_size)
        values = scaled[:, span]
        parts = []
        for h in (2 * pair, 2 * pair + 1):
            decay = jnp.exp2(jnp.minimum(run_q[:, h : h + 1] - run_t[0, h : h + 1], 0.0))
            parts.append(nn((scores * decay).astype(LOW), values))
        inner_o[:, span] = jnp.where(lane < head_size, parts[0], parts[1])

    @pl.when(at == 0)
    def _():
        for load in loads:
            load.wait()

    gate_o[...] = nn(normed[...], proj[...])
    masked = (labels.valid() * cot[...].astype(F32)).astype(LOW)
    masked_o[...] = masked
    back_o[...] = nt(masked, out_proj[...]) * gain[...]


def gate_step(
    sizes, info, hid, masked_back, gate, inner, values, maps, run, state, carry, out_proj, gain,
    block_o, gated_o, back_o, enter_back_o, gate_back_o, row_o, out_back_o, enter_o,
    now, leaving, through, skip_row, entry, scan, unit_buf, slope_buf, gain_buf, skip_sum, prod_high, prod_rest, back_rest,
    at,
):
    inner_width, channels, heads = sizes
    state_size = (channels - inner_width) // 2
    labels = Labels(info, at)
    groups = head_groups(heads, inner_width)
    pairs = head_groups(heads, inner_width, 2)
    out_map = maps[:, state_size:]
    entry[...] = spread(labels.entry() * jnp.exp2(run[...]), pairs)
    entering = now[...]
    enter_o[0] = entering
    enter_high, enter_rest = halves(entering)
    scan[...] = nn(out_map, enter_high)
    factor = carry[0, 0:1]
    now[...] = factor * entering + state[0]
    valid = labels.valid()
    rates = []
    for here in bands():
        squares = jnp.zeros((BAND, 128), F32)
        for cols in columns_of(inner_width):
            scanned = inner[here, cols] + entry[here, cols] * scan[here, cols]
            inner[here, cols] = scanned
            mixer = scanned + skip_row[0:1, cols] * values[here, cols]
            scan[here, cols] = mixer
            si, slope = silu_parts(gate[here, cols])
            gate[here, cols] = si
            slope_buf[here, cols] = slope
            gated = mixer * si
            unit_buf[here, cols] = gated
            squares += gated * gated
        rate = lax.rsqrt(jnp.sum(squares, axis=1, keepdims=True) * (1.0 / inner_width) + EPS)
        rate = jnp.broadcast_to(rate, (BAND, 128))
        rates.append(rate)
        for cols in columns_of(inner_width):
            unit = unit_buf[here, cols] * rate
            unit_buf[here, cols] = unit
            gated_o[here, cols] = (unit * gain[:, cols]).astype(LOW)
    branch = nn(gated_o[...], out_proj[...])
    block_o[...] = (valid * (hid[...].astype(F32) + branch)).astype(LOW)
    for here, rate in zip(bands(), rates):
        means = jnp.zeros((BAND, 128), F32)
        for cols in columns_of(inner_width):
            product = masked_back[here, cols] * unit_buf[here, cols]
            gain_buf[:, cols] += fold_rows(product)
            means += product
        mean = jnp.sum(means, axis=1, keepdims=True) * (1.0 / inner_width)
        mean = jnp.broadcast_to(mean, (BAND, 128))
        for cols in columns_of(inner_width):
            gated_back = rate * (masked_back[here, cols] - unit_buf[here, cols] * mean)
            gate_back_o[here, cols] = (gated_back * scan[here, cols] * slope_buf[here, cols]).astype(LOW)
            mixer_back = gated_back * gate[here, cols]
            skip_sum[:, cols] += fold_rows(mixer_back * values[here, cols])
            back_low = mixer_back.astype(LOW)
            back_o[here, cols] = back_low
            prod_high[here, cols], prod_rest[here, cols] = halves(back_low.astype(F32) * inner[here, cols])
            enter_back_o[here, cols], back_rest[here, cols] = halves(entry[here, cols] * mixer_back)
    row_o[...] = nt(prod_high[...], groups) + nt(prod_rest[...], groups)
    back_high = enter_back_o[...]
    both = nt(back_high, jnp.concatenate([enter_high, enter_rest], axis=0))
    out_back_o[...] = both[:, :state_size] + both[:, state_size:] + nt(back_rest[...], enter_high)
    leaving[...] += through[0:1] * tn(out_map, back_high)
    through[...] = through[...] * factor


def back_kernel(
    sizes, count, info, maps, scaled, back, run, run_t, gated_in, masked_in, normed_in, gate_back_in, leaving, through,
    pre_in, enter_back_in, out_in, row_in, step, sig, enter_in, carry, mixed_in, mixed_tail, rows, a_log, skip,
    inner_gain_sum, skip_sum,
    late_o, late_halo_o, sums_o, out_sum_o, gate_sum_o,
    gated, masked, normed, gate_back, load_sem, pre_buf, pre_sem, enter_back_buf, enter_back_sem, enter_buf, enter_sem,
    mixed_buf, mixed_sem,
    values_all, maps_all, col_all, out_grad, gate_grad,
    state, ext, skip_row, same_buf, steps_wide, tails_wide, from_state, tail_low, col_low, step_low, sum_buf,
    *scratch
):
    inner_width, channels, heads = sizes
    turn = pl.program_id(0)
    me = Place()
    exchange = Exchange(True, lambda: head_groups(heads, inner_width, 2), leaving, through, *scratch[:EXCHANGE_BUFFERS])
    scratch = scratch[EXCHANGE_BUFFERS:]
    bufs = [scratch[SCATTER_BUFFERS * a : SCATTER_BUFFERS * (a + 1)] for a in range(2)]
    scatter = Scatter(me, [out_grad, gate_grad], bufs, *scratch[2 * SCATTER_BUFFERS :])
    points = [
        Points(scatter.stages(0), [place * count // 4 for place in (6, 8, 12, 14)], 3),
        Points(scatter.stages(1), [place * count // 4 for place in (12, 14, 18, 20)], 3),
    ]

    def hook(number):
        for one in points:
            one.hook(number)

    loads = [
        pltpu.make_async_copy(source, target, load_sem.at[k])
        for k, (source, target) in enumerate(
            ((gated_in, gated), (masked_in, masked), (normed_in, normed), (gate_back_in, gate_back))
        )
    ]
    streams = [
        Stream(pre_in, pre_buf, pre_sem), Stream(enter_back_in, enter_back_buf, enter_back_sem),
        Stream(enter_in, enter_buf, enter_sem), Stream(mixed_in, mixed_buf, mixed_sem),
    ]

    @pl.when(turn == 0)
    def _():
        for load in loads:
            load.start()
        greet(exchange.others() + [me.device(x=p) for _, p in me.peers("x")] + [me.twin])
        exchange.start()

    pl.when(turn == count // 2)(exchange.middle)
    half = count // 2
    wide = inner_width // half

    hook(0)

    @pl.when(turn < count)
    def _():
        inner_back_step(
            sizes, info, maps, scaled, back, run, run_t, values_all.at[turn], maps_all.at[turn], col_all.at[turn], turn,
            hook,
        )

    cols = pl.ds(pl.multiple_of(lax.rem(turn, half) * wide, wide), wide)

    @pl.when(turn < half)
    def _():
        @pl.when(turn == 0)
        def _():
            loads[0].wait()
            loads[1].wait()

        grad = tn(gated[:, cols], masked[...])
        size = out_grad.shape[2]
        each = me.count // half
        for q in range(each):
            at = turn * (each // me.seqs) + q // me.seqs
            out_grad[at, q % me.seqs] = grad[q * size : (q + 1) * size].astype(LOW)

    @pl.when((turn >= half) & (turn < count))
    def _():
        @pl.when(turn == half)
        def _():
            loads[2].wait()
            loads[3].wait()

        grad = tn(normed[...], gate_back[:, cols])
        size = gate_grad.shape[2]
        for q in range(me.count):
            gate_grad[q // me.seqs, q % me.seqs, :, cols] = grad[q * size : (q + 1) * size].astype(LOW)

    @pl.when(turn == count - 1)
    def _():
        for stream in streams:
            stream.start(count - 1, 0)

    @pl.when(turn == count)
    def _():
        exchange.finish()
        state[...] = exchange.landed()
        ext[0:EDGE] = jnp.zeros((EDGE, channels), F32)
        ext[EDGE + BLOCK :] = jnp.zeros((EDGE, channels), F32)
        sums_o[...] = jnp.zeros_like(sums_o)
        sum_buf[...] = jnp.zeros_like(sum_buf)
        skip_row[...] = spread(jnp.broadcast_to(skip[...], (8, heads)), head_groups(heads, inner_width, 2))

    @pl.when(turn >= count)
    def _():
        at = 2 * count - 1 - turn
        slot = lax.rem(turn - count, 2)
        for stream in streams:
            stream.wait(slot)

        @pl.when(at > 0)
        def _():
            for stream in streams:
                stream.start(at - 1, 1 - slot)

        pre, enter_back, enter, mixed = (stream.buf.at[slot] for stream in streams)
        finish_step(
            sizes, info, pre, maps, scaled, back, enter_back, values_all.at[at], maps_all.at[at], out_in, col_all.at[at],
            row_in, step, run, sig, enter, carry, mixed, mixed_tail, rows, a_log, inner_gain_sum, skip_sum,
            late_o, late_halo_o, sums_o,
            state, ext, skip_row, same_buf, steps_wide, tails_wide, from_state, tail_low, col_low, step_low, sum_buf,
            at, hook,
        )

    @pl.when(turn == 2 * count - 1)
    def _():
        for a, out in enumerate((out_sum_o, gate_sum_o)):
            out[...] = scatter.result(a)
        scatter.settle()


def inner_back_step(sizes, info, maps, scaled, back, run, run_t, values_o, maps_o, col_o, at, hook):
    inner_width, channels, heads = sizes
    state_size = (channels - inner_width) // 2
    head_size = inner_width // heads
    labels = Labels(info, at)
    in_map = maps[:, :state_size]
    out_map = maps[:, state_size:]
    s_at = lax.broadcasted_iota(jnp.int32, (BLOCK, BLOCK), 0)
    q_at = lax.broadcasted_iota(jnp.int32, (BLOCK, BLOCK), 1)
    inside = (q_at >= s_at) & (labels.column() == labels.row())
    scores = jnp.where(inside, nt(in_map, out_map), 0.0)
    lane = lax.broadcasted_iota(jnp.int32, (BLOCK, 2 * head_size), 1)
    run_s = run[...]
    total = jnp.zeros((BLOCK, BLOCK), F32)
    for pair in range(heads // 2):
        if pair in (heads // 6, heads // 3):
            hook(pair * 6 // heads)
        span = slice(pair * 2 * head_size, (pair + 1) * 2 * head_size)
        values = scaled[:, span]
        grad = back[:, span]
        parts = []
        for h in (2 * pair, 2 * pair + 1):
            mine = (lane < head_size) == (h % 2 == 0)
            decay = jnp.exp2(jnp.minimum(run_t[0, h : h + 1] - run_s[:, h : h + 1], 0.0))
            parts.append(nn((scores * decay).astype(LOW), grad))
            total += decay * nt(jnp.where(mine, values, jnp.zeros_like(values)), grad)
        values_o[:, span] = jnp.where(lane < head_size, parts[0], parts[1])
    total = jnp.where(inside, total, 0.0).astype(LOW)
    maps_o[:, :state_size] = nn(total, out_map)
    maps_o[:, state_size:] = tn(total, in_map)
    col_o[...] = head_sums(values_o[...] * scaled[...].astype(F32), head_groups(heads, inner_width))


def finish_step(
    sizes, info, pre, maps, scaled, back, enter_back, values_in, maps_in, out_in, col_in, row_in, step, run, sig, enter,
    carry, mixed, mixed_tail, rows, a_log, inner_gain_sum, skip_sum,
    late_o, late_halo_o, sums_o,
    state, ext, skip_row, same_buf, steps_wide, tails_wide, from_state, tail_low, col_low, step_low, sum_buf,
    at, hook,
):
    inner_width, channels, heads = sizes
    state_size = (channels - inner_width) // 2
    labels = Labels(info, at)
    group = head_groups(heads, inner_width)
    pairs = head_groups(heads, inner_width, 2)
    in_map = maps[:, :state_size]
    out_map = maps[:, state_size:]
    run_q = run[...]
    steps = step[...]
    tails_wide[...] = spread(labels.keep() * jnp.exp2(run_q[BLOCK - 1 :] - run_q), pairs)
    steps_wide[...] = spread(steps, pairs)
    state_low = state[...].astype(LOW)
    from_state[...] = nn(in_map, state_low)
    same = Labels(info, at, BLOCK + EDGE).same()
    wide_columns(same, 4, same_buf)
    for here in bands():
        for cols in columns_of(inner_width):
            tail = tails_wide[here, cols]
            scaled_f = scaled[here, cols].astype(F32)
            tail_low[here, cols] = (tail * scaled_f).astype(LOW)
            from_tail = tail * from_state[here, cols]
            col_low[here, cols] = (scaled_f * from_tail).astype(LOW)
            scaled_back = values_in[here, cols] + from_tail
            act, slope = silu_parts(pre[here, cols])
            step_low[here, cols] = (act * scaled_back).astype(LOW)
            values_back = steps_wide[here, cols] * scaled_back + skip_row[0:1, cols] * back[here, cols].astype(F32)
            ext[shifted(here, EDGE), cols] = values_back * slope
    hook(1)
    col_tail = nt(col_low[...], group)
    step_back = nt(step_low[...], group)
    in_back = maps_in[:, :state_size] + nt(tail_low[...], state_low)
    out_back = maps_in[:, state_size:] + out_in[...]
    factor = carry[0, 0:1]
    shared = jnp.sum(enter[0] * state[...], axis=0, keepdims=True) * factor
    shared = row_sums(shared, group)
    state[...] = factor * state[...] + tn(out_map, enter_back[...])
    order = triangle()
    decay_back = (
        tn(order, row_in[...] - col_in[...], HIGHEST) + nn(order, col_tail, HIGHEST) - col_tail + shared
    )
    rate_row = jnp.exp(a_log[...])
    sums_o[7:8, 0:heads] += jnp.sum(decay_back * steps, axis=0, keepdims=True) * -rate_row
    raw_back = (step_back - rate_row * decay_back) * sig[...]
    sums_o[7:8, 128 : 128 + heads] += jnp.sum(raw_back, axis=0, keepdims=True)
    raw_low = raw_back.astype(LOW)
    late_o[:, channels:] = raw_low
    _, slope = silu_parts(pre[:, inner_width:])
    ext[EDGE : EDGE + BLOCK, inner_width : inner_width + state_size] = in_back * slope[:, :state_size]
    ext[EDGE : EDGE + BLOCK, inner_width + state_size :] = out_back * slope[:, state_size:]
    hook(2)
    for cols in columns_of(channels):
        sums = [jnp.zeros((8, 128), F32) for _ in range(5)]
        for here in bands():
            pre_back = ext[shifted(here, EDGE), cols]
            inputs = mixed[here, cols]
            total = rows[3:4, cols] * pre_back
            sums[4] += fold_rows(pre_back)
            sums[3] += fold_rows(pre_back * inputs)
            for j in (1, 2, 3):
                ahead = same_buf[j, shifted(here, j)] * ext[shifted(here, EDGE + j), cols]
                sums[3 - j] += fold_rows(ahead * inputs)
                total += rows[3 - j : 4 - j, cols] * ahead
            late_o[here, cols] = total.astype(LOW)
        for k in range(5):
            sum_buf[k, :, cols] += sums[k]
    ext[EDGE + BLOCK :] = ext[EDGE : 2 * EDGE]

    @pl.when(at == 0)
    def _():
        padded = jnp.concatenate([jnp.zeros((EDGE, 8), F32), same[:EDGE]], axis=0)
        edge = jnp.zeros((EDGE, channels), F32)
        for j in (1, 2, 3):
            ahead = padded[j : j + EDGE, j : j + 1] * ext[j : j + EDGE]
            sum_buf[3 - j] += ahead * mixed_tail[0]
            edge += rows[3 - j : 4 - j] * ahead
        edge_low = jnp.concatenate([jnp.zeros((HALO - EDGE, channels), F32), edge], axis=0).astype(LOW)
        late_halo_o[:, :channels] = edge_low
        late_halo_o[:, channels:] = jnp.zeros((HALO, heads), LOW)
        for k in range(5):
            sums_o[k : k + 1] = jnp.sum(sum_buf[k], axis=0, keepdims=True)
        sums_o[5:6, :inner_width] = inner_gain_sum[...]
        sums_o[7:8, 256 : 256 + heads] = row_sums(skip_sum[...], group)


def last_kernel(
    sizes, normed_in, normed_halo, late_in, late_halo, gate_sum, sums, gain, halo, hid_in, masked_in, gate_back_in,
    gate_proj_in, late_proj_in, proj_o, small_o, hid_o,
    normed, late, hid, masked, gate_back, gate_proj, late_proj, load_sem, halo_hid, halo_buf, halo_sem, small_buf, small_sem, grads,
    *scratch
):
    inner_width, channels, heads = sizes
    me = Place()
    bufs = scratch[:SCATTER_BUFFERS]
    scatter = Scatter(me, [grads], [bufs], *scratch[SCATTER_BUFFERS:])
    loads = [
        pltpu.make_async_copy(source, target, load_sem.at[k])
        for k, (source, target) in enumerate(
            (
                (normed_in, normed), (late_in, late), (late_proj_in, late_proj), (gate_proj_in, gate_proj), (gate_back_in, gate_back), (hid_in, hid),
                (masked_in, masked),
            )
        )
    ]
    for load in loads:
        load.start()
    greet(me.around() + [me.along(1), me.along(-1)])
    back = remote(halo_hid, halo_buf, halo_sem.at[0], halo_sem.at[1], me.along(-1))

    axes = [
        (CORES, me.core, [(1, 1 - me.core, me.twin)]),
        (me.sx, me.x, [(k, p, me.device(x=p)) for k, p in me.peers("x")]),
        (me.sy, me.y, [(k, p, me.device(y=p)) for k, p in me.peers("y")]),
        (me.sz, me.z, [(k, p, me.device(z=p)) for k, p in me.peers("z")]),
    ]

    def small_copies(stage):
        _, mine, peers = axes[stage]
        buf = small_buf.at[stage, mine]
        return [remote(buf, buf, small_sem.at[0, stage, k], small_sem.at[1, stage, mine], device) for k, _, device in peers]

    def small_send(stage, value):
        small_buf[stage, axes[stage][1]] = value
        for copy in small_copies(stage):
            copy.start()

    def small_take(stage):
        size, _, peers = axes[stage]
        for _, p, _ in peers:
            buf = small_buf.at[stage, p]
            remote(buf, buf, small_sem.at[0, stage, 0], small_sem.at[1, stage, p], me.twin).wait_recv()
        total = small_buf[stage, 0]
        for i in range(1, size):
            total = total + small_buf[stage, i]
        return total

    for load in loads[:2]:
        load.wait()
    own_rows = normed.shape[1] // me.count
    half = me.seqs * own_rows
    for x in range(me.sx):
        span = slice(2 * half * x, 2 * half * (x + 1))
        grad = tn(normed[:, span], late[...]) + tn(normed_halo[:, span], late_halo[...])
        for q in range(CORES * me.seqs):
            grads[x * CORES + q // me.seqs, q % me.seqs] = grad[q * own_rows : (q + 1) * own_rows].astype(LOW)
        for group in range(me.sz):
            scatter.copies(0, 0, group, x)[0].start()
    gain_row = gain[...]

    def norm_back(normed_back, v):
        rate = rms_rate(v)
        unit = v * rate
        product = normed_back * unit
        mean = jnp.mean(product * gain_row, axis=-1, keepdims=True)
        return rate * (normed_back * gain_row - unit * mean), jnp.sum(product, axis=0, keepdims=True)

    for load in loads[2:]:
        load.wait()
    edge, gain_sum = norm_back(nt(late_halo[:, :channels], late_proj[:, :channels]), halo[...].astype(F32))
    halo_hid[...] = edge
    back.start()
    blocks = hid.shape[0] // BLOCK
    def take(stage, groups):
        for group in groups:
            scatter.absorb(0, stage, group)

    early, later = range(me.sz // 2), range(me.sz // 2, me.sz)
    for block in range(blocks):
        here = slice(block * BLOCK, (block + 1) * BLOCK)
        normed_back = nt(gate_back[here], gate_proj[...]) + nt(late[here], late_proj[...])
        rows_back, more = norm_back(normed_back, hid[here].astype(F32))
        gain_sum += more
        result = masked[here].astype(F32) + rows_back
        if block < blocks - 1:
            hid_o[here] = result.astype(LOW)
        if block == 0:
            take(0, early)
        if block == blocks // 2 - 1:
            take(0, later)
    take(1, early)
    small_buf[0, me.core] = sums[...]
    small_buf[0, me.core, 6:7, 0 : normed.shape[1]] = gain_sum
    small_send(0, small_buf[0, me.core])
    small_send(1, small_take(0))
    take(1, later)
    take(2, early)
    small_send(2, small_take(1))
    take(2, later)
    small_send(3, small_take(2))
    back.wait()
    returned = jnp.where(me.seq < me.seqs - 1, halo_buf[...], 0.0)
    hid_o[hid.shape[0] - BLOCK : hid.shape[0] - HALO] = result[: BLOCK - HALO].astype(LOW)
    hid_o[hid.shape[0] - HALO :] = (result[BLOCK - HALO :] + returned).astype(LOW)
    total = small_take(3)
    mine_at = me.row * me.seqs + me.seq

    def own(v, size):
        width = v.shape[1]
        return pltpu.roll(v, lax.rem(width - mine_at * size, width), 1)[:, :size]

    part = channels // me.count
    small_o[0:5, 0:part] = own(total, part)[0:5]
    inner_part = inner_width // me.count
    small_o[5:6, 0:inner_part] = own(total, inner_part)[5:6]
    small_o[6:7, 0:own_rows] = own(total, own_rows)[6:7]
    for k in range(3):
        small_o[7 + k : 8 + k, 0:heads] = total[7:8, 128 * k : 128 * k + heads]
    proj_o[:, :inner_width] = gate_sum[...]
    proj_o[:, inner_width:] = scatter.result(0)
    scatter.settle()
    for stage in range(4):
        for copy in small_copies(stage):
            copy.wait_send()


def tidy_kernel(
    proj, out, small, hid_grad, block, proj_o, out_o, taps_o, offset_o, inner_gain_o, gain_o, a_log_o, dt_bias_o, skip_o,
    hid_o, block_o,
):
    hid_o[...] = hid_grad[...]
    block_o[...] = block[...]
    proj_o[...] = proj[...]
    out_o[...] = out[...]
    width, part = taps_o.shape
    taps_o[...] = small[0:width, 0:part]
    for k, ref in enumerate((offset_o, inner_gain_o, gain_o, a_log_o, dt_bias_o, skip_o)):
        ref[...] = small[width + k, 0 : ref.shape[0]]


def struct(shape, dtype=F32):
    return jax.ShapeDtypeStruct(shape, dtype)


def run_kernel(kernel, name, count, ins, outs, scratch=(), flip=False, collective_id=None, aliases=None, before=0):
    def block(i):
        if before:
            return jnp.maximum(i - before, 0)
        return count - 1 - i if flip else i

    def spec(array, kind):
        shape = array.shape
        zeros = (0,) * (len(shape) - 1)
        if kind == "any":
            return pl.BlockSpec(memory_space=pl.ANY)
        if kind == "scalar":
            return pl.BlockSpec(memory_space=pltpu.SMEM)
        if kind == "w":
            return pl.BlockSpec(shape, lambda i: (0,) + zeros)
        if kind == "once":
            return pl.BlockSpec(shape, lambda i: (0,) + zeros, pipeline_mode=pl.Buffered(1))
        if kind == "r":
            return pl.BlockSpec((BLOCK,) + shape[1:], lambda i: (block(i),) + zeros)
        if kind == "b":
            return pl.BlockSpec((1,) + shape[1:], lambda i: (block(i),) + zeros)
        base, place = kind[0], kind[-1]
        if base == "r":
            return pl.BlockSpec((BLOCK,) + shape[1:], lambda i: (place(i),) + zeros)
        if base == "b":
            return pl.BlockSpec((1,) + shape[1:], lambda i: (place(i),) + zeros)
        return pl.BlockSpec((shape[0], shape[1] // kind[1]), lambda i: (0, place(i)))

    return pl.pallas_call(
        kernel,
        name=name,
        grid=(count + before,),
        in_specs=[spec(a, k) for a, k in ins],
        out_specs=[spec(a, k) for a, k in outs],
        out_shape=[a for a, _ in outs],
        scratch_shapes=list(scratch),
        input_output_aliases=aliases or {},
        compiler_params=pltpu.CompilerParams(
            dimension_semantics=("arbitrary",),
            vmem_limit_bytes=VMEM_BYTES,
            collective_id=collective_id,
            has_side_effects=collective_id is not None,
        ),
    )(*[a for a, _ in ins])


def body(
    hidden, lengths, cotangent, norm_gain, in_proj, conv_weight, conv_bias, a_log, dt_bias, skip_weight, inner_gain,
    out_proj,
):
    length, model = hidden.shape[1:]
    count = length // BLOCK
    heads = a_log.shape[0]
    devices = lax.axis_size(AXES)
    seqs = lax.axis_size("seq")
    inner_width = out_proj.shape[0] * devices
    channels = conv_weight.shape[1] * devices
    state_size = (channels - inner_width) // 2
    sizes = (inner_width, channels, heads)
    hid = hidden[0]
    cot = cotangent[0]
    width, part = conv_weight.shape
    own_rows, columns = in_proj.shape
    a_row, bias_row, skip_row = a_log[None], dt_bias[None], skip_weight[None]
    info = jnp.concatenate([lengths, (lax.axis_index("seq") * length).reshape(1, 1)], axis=1)

    late_width = columns - inner_width
    late_width = columns - inner_width
    token = struct((length, inner_width), LOW)
    (
        normed, normed_halo, pre, values, maps, scaled, mixed, mixed_tail, step, run, run_t, sig, state, carry, final_state,
        through, late_proj, rows, inner_gain_row, gain_row, halo, gate_all, out_all,
    ) = run_kernel(
        functools.partial(project_kernel, sizes, count), "project", count,
        [
            (info, "scalar"), (hid, "r"), (hid, "any"), (a_row, "w"), (bias_row, "w"), (in_proj, "any"), (out_proj, "any"),
            (conv_weight, "w"), (conv_bias[None], "w"), (inner_gain[None], "w"), (norm_gain[None], "w"),
        ],
        [
            (struct((length, model), LOW), "r"), (struct((HALO, model), LOW), "w"),
            (struct((length, channels)), "r"), (struct((length, inner_width)), "r"),
            (struct((length, 2 * state_size), LOW), "r"), (token, "r"), (struct((length, channels)), "r"),
            (struct((count, EDGE, channels)), "b"), (struct((length, heads)), "r"), (struct((length, heads)), "r"),
            (struct((count, heads, BLOCK)), "b"), (struct((length, heads)), "r"),
            (struct((count, state_size, inner_width)), "b"), (struct((count, 8, inner_width)), "b"),
            (struct((state_size, inner_width), LOW), "w"), (struct((8, 128)), "w"),
            (struct((model, late_width), LOW), "w"), (struct((8, channels)), "w"), (struct((1, inner_width)), "w"),
            (struct((1, model)), "w"), (struct((HALO, model), LOW), "w"),
            (struct((devices, own_rows, inner_width), LOW), "any"), (struct((devices,) + out_proj.shape, LOW), "any"),
        ],
        [
            pltpu.VMEM((EDGE + BLOCK, channels), F32), pltpu.VMEM((state_size, inner_width), F32),
            pltpu.VMEM((8, 128), F32), pltpu.VMEM((BLOCK, inner_width), F32), pltpu.VMEM((BLOCK, inner_width), F32),
            pltpu.VMEM((BLOCK, inner_width), LOW), pltpu.VMEM((4, BLOCK, 128), F32),
            pltpu.VMEM((8, 128), F32), pltpu.VMEM((devices, 8, 128), F32),
            pltpu.VMEM((devices, own_rows, late_width), LOW), pltpu.VMEM((HALO, model), LOW), pltpu.SemaphoreType.DMA((2,)),
        ] + gather_semaphores(2) + gather_semaphores(2),
        collective_id=1,
        before=1,
    )
    out_full = out_all.reshape(inner_width, model)
    gate_proj = gate_all.reshape(model, inner_width)
    pieces = (seqs, state_size // seqs, inner_width)
    blocks = (count, BLOCK, inner_width)
    def ahead(i):
        return jnp.minimum(i, count - 1)

    def after(i):
        return jnp.maximum(i - count, 0)

    def twice(i):
        return jnp.where(i < count, i, i - count)

    def there(i):
        return jnp.where(i < count, i, 2 * count - 1 - i)

    def back_again(i):
        return jnp.where(i < count, count - 1, 2 * count - 1 - i)

    (
        masked, block_out, gated, back, enter_back, gate_back, row_term, out_in, enter, leaving, inner_gain_sum, skip_sum,
    ) = run_kernel(
        functools.partial(mix_kernel, sizes, count), "mix", 2 * count,
        [
            (info, "scalar"), (normed, ("r", ahead)), (gate_proj, "any"), (out_full, "any"), (inner_gain_row, "w"),
            (cot, ("r", ahead)), (maps, ("r", twice)), (scaled, ("r", ahead)), (run, ("r", twice)),
            (run_t, ("b", ahead)), (final_state.reshape(pieces), "once"), (through, "w"),
            (hid, "any"), (values, "any"), (state, "any"), (carry, ("b", after)), (skip_row, "w"),
        ],
        [
            (struct((length, model), LOW), ("r", ahead)), (struct((length, model), LOW), ("r", after)),
            (token, ("r", after)), (token, ("r", after)), (token, ("r", after)), (token, ("r", after)),
            (struct((length, heads)), ("r", after)), (struct((length, state_size)), ("r", after)),
            (struct((count, state_size, inner_width)), ("b", after)), (struct((state_size, inner_width), LOW), "w"),
            (struct((1, inner_width)), "w"), (struct((1, inner_width)), "w"),
        ],
        [
            pltpu.VMEM(gate_proj.shape, LOW), pltpu.VMEM(out_full.shape, LOW), pltpu.SemaphoreType.DMA((2,)),
        ]
        + stream_scratch(hid) + stream_scratch(values) + stream_scratch(state)
        + [pltpu.VMEM(blocks, F32)] * 3
        + [
            pltpu.VMEM((state_size, inner_width), F32), pltpu.VMEM((state_size, inner_width), F32),
            pltpu.VMEM((8, inner_width), F32), pltpu.VMEM((8, inner_width), F32),
        ]
        + [pltpu.VMEM((BLOCK, inner_width), F32)] * 4
        + [pltpu.VMEM((8, inner_width), F32)] * 2
        + [pltpu.VMEM((BLOCK, inner_width), LOW)] * 3
        + exchange_scratch(pieces),
        collective_id=2,
    )
    gate_one = (own_rows, inner_width)
    late, late_halo, sums, out_sum, gate_sum = run_kernel(
        functools.partial(back_kernel, sizes, count), "back", 2 * count,
        [
            (info, "scalar"), (maps, ("r", there)), (scaled, ("r", there)), (back, ("r", there)), (run, ("r", there)),
            (run_t, ("b", ahead)), (gated, "any"), (masked, "any"), (normed, "any"), (gate_back, "any"),
            (leaving.reshape(pieces), "once"), (through, "w"),
            (pre, "any"), (enter_back, "any"), (out_in, ("r", back_again)),
            (row_term, ("r", back_again)), (step, ("r", back_again)), (sig, ("r", back_again)),
            (enter, "any"), (carry, ("b", back_again)), (mixed, "any"),
            (mixed_tail, ("b", back_again)), (rows, "w"), (a_row, "w"), (skip_row, "w"), (inner_gain_sum, "w"),
            (skip_sum, "w"),
        ],
        [
            (struct((length, late_width), LOW), ("r", back_again)), (struct((HALO, late_width), LOW), "w"),
            (struct((8, channels)), "w"), (struct(out_proj.shape), "w"), (struct(gate_one), "w"),
        ],
        [
            pltpu.VMEM(gated.shape, LOW), pltpu.VMEM(masked.shape, LOW), pltpu.VMEM(normed.shape, LOW),
            pltpu.VMEM(gate_back.shape, LOW), pltpu.SemaphoreType.DMA((4,)),
        ]
        + stream_scratch(pre) + stream_scratch(enter_back) + stream_scratch(enter) + stream_scratch(mixed)
        + [
            pltpu.VMEM(blocks, F32), pltpu.VMEM((count, BLOCK, 2 * state_size), F32), pltpu.VMEM((count, BLOCK, heads), F32),
            pltpu.VMEM((devices // seqs, seqs) + out_proj.shape, LOW), pltpu.VMEM((devices // seqs, seqs) + gate_one, LOW),
            pltpu.VMEM((state_size, inner_width), F32), pltpu.VMEM((2 * EDGE + BLOCK, channels), F32),
            pltpu.VMEM((8, inner_width), F32), pltpu.VMEM((4, BLOCK + EDGE, 128), F32),
        ]
        + [pltpu.VMEM((BLOCK, inner_width), F32)] * 3
        + [pltpu.VMEM((BLOCK, inner_width), LOW)] * 3
        + [pltpu.VMEM((5, 8, channels), F32)]
        + exchange_scratch(pieces)
        + scatter_scratch([out_proj.shape, gate_one]),
        collective_id=3,
    )
    late_one = (own_rows, late_width)
    most = max(CORES, lax.axis_size("row") // CORES, DEPTH, seqs // DEPTH)
    proj_sum, small_sums, hid_grad = run_kernel(
        functools.partial(last_kernel, sizes), "last", 1,
        [
            (normed, "any"), (normed_halo, "w"), (late, "any"), (late_halo, "w"), (gate_sum, "w"), (sums, "w"),
            (gain_row, "w"), (halo, "w"), (hid, "any"), (masked, "any"), (gate_back, "any"), (gate_proj, "any"),
            (late_proj, "any"),
        ],
        [(struct(in_proj.shape), "w"), (struct((16, 128)), "w"), (struct((length, model), LOW), "w")],
        [
            pltpu.VMEM(normed.shape, LOW), pltpu.VMEM(late.shape, LOW), pltpu.VMEM(hid.shape, LOW),
            pltpu.VMEM(hid.shape, LOW), pltpu.VMEM(gate_back.shape, LOW), pltpu.VMEM(gate_proj.shape, LOW),
            pltpu.VMEM(late_proj.shape, LOW), pltpu.SemaphoreType.DMA((7,)),
            pltpu.VMEM((HALO, model), F32), pltpu.VMEM((HALO, model), F32), pltpu.SemaphoreType.DMA((2,)),
            pltpu.VMEM((4, most, 8, channels), F32),
            pltpu.SemaphoreType.DMA((2, 4, most)), pltpu.VMEM((devices // seqs, seqs) + late_one, LOW),
        ] + scatter_scratch([late_one]),
        collective_id=5,
    )
    proj_grad, out_proj_grad, taps_grad, offset_grad, inner_grad, gain_grad, a_log_grad, dt_grad, skip_grad, hid_grad, block_out = (
        run_kernel(
            tidy_kernel, "tidy", count,
            [(proj_sum, "once"), (out_sum, "once"), (small_sums, "w"), (hid_grad, "r"), (block_out, "r")],
            [
                (struct(in_proj.shape), "w"), (struct(out_proj.shape), "w"), (struct((width, part)), "w"),
                (struct((part,)), "w"), (struct(inner_gain.shape), "w"), (struct(norm_gain.shape), "w"),
                (struct((heads,)), "w"), (struct((heads,)), "w"), (struct((heads,)), "w"),
                (struct((length, model), LOW), "r"), (struct((length, model), LOW), "r"),
            ],
        )
    )
    return (
        block_out[None], hid_grad[None], gain_grad, proj_grad, taps_grad, offset_grad, a_log_grad, dt_grad, skip_grad,
        inner_grad, out_proj_grad,
    )


def solution(mesh):
    weights = P(AXES)
    tokens = P("row", "seq", None)
    rows = P(AXES, None)
    return jax.shard_map(
        body,
        mesh=mesh,
        in_specs=(
            tokens, P("row", None), tokens, weights, rows, P(None, AXES), weights, P(), P(), P(), weights, rows,
        ),
        out_specs=(tokens, tokens, weights, rows, P(None, AXES), weights, P(), P(), P(), weights, rows),
        check_vma=False,
    )
```
